128 devices in a mesh: view: 4 (over x_hi, core), col: 32 (over y, z, x_lo).
Axes of the slice: x: 4 (x_hi: 2, x_lo: 2; x = x_hi * 2 + x_lo), y: 4, z: 4, core: 2. Of those that a mesh axis runs over, the one named last changes fastest.
Arguments:
- views: bfloat16 [64, 1024, 2048], P('view', 'col'), may hold values from 0.099609375 to 1
- phases: int32 [64, 64], replicated, may hold values from 0 to 255
- kernel_phase: float32 [65536], replicated, may hold values from -3.140625 to 3.140625
Outputs:
- propagated_re: float32 [2048, 65536], P(('view', 'col'))
- propagated_im: float32 [2048, 65536], P(('view', 'col'))
The draws below stay inside these ranges and needn't reach their ends.
All inputs are finite; a program needn't handle non-finite values.
Results may differ from the reference program's by a relative error of at most 0.0057.
Values may be sent and summed in bfloat16 or wider, within the bound.
No kernel may reach another device: no remote copies, remote signals or barrier semaphores. Data moves between devices by JAX's collectives and lax.ppermute only.
A program may use at most 128 MiB of HBM per device.

```python
import math
import jax
import jax.numpy as jnp
from jax import lax

DIRS = 64
HOG_COLS = 1024
PHASES = 256
HROWS = 32
ROWS = 2048
WIDTH = 65536


def with_ends(drawn, key, smallest, largest):
    place = [jax.random.randint(jax.random.fold_in(key, axis), (), 0, length) for axis, length in enumerate(drawn.shape)]
    widest = drawn.shape.index(max(drawn.shape))
    beside = place[:widest] + [(place[widest] + 1) % drawn.shape[widest]] + place[widest + 1:]
    return drawn.at[tuple(place)].set(smallest).at[tuple(beside)].set(largest)


def shard_levels(own_key, extent, shards, low, high):
    def one(dim, shards_of):
        heights = jax.random.uniform(jax.random.fold_in(jax.random.fold_in(own_key, 6), dim), (shards_of,), jnp.float32, low / len(shards), high / len(shards))
        return jnp.repeat(jnp.exp(heights), extent[dim] // shards_of).reshape((-1,) + (1,) * (len(extent) - dim - 1))

    gain = one(*shards[0])
    for cut in shards[1:]:
        gain = gain * one(*cut)
    return gain


def setup_inputs(seed: int = 0) -> dict:
    keys = jax.random.split(jax.random.key(seed), 4)
    return {
        "views": jnp.clip(0.099609375 + 0.9003906 * jax.random.uniform(keys[0], (DIRS, HOG_COLS, HROWS * DIRS), jnp.float32) ** shard_levels(keys[0], (DIRS, HOG_COLS, HROWS * DIRS), ((0, 4), (1, 32)), -0.2, 0.2), 0.099609375, 1.0).astype(jnp.bfloat16),
        "phases": with_ends(jax.random.randint(keys[1], (DIRS, DIRS), 0, PHASES), jax.random.fold_in(keys[1], 1), 0, PHASES - 1).astype(jnp.int32),
        "kernel_phase": jnp.clip(jax.random.uniform(keys[2], (WIDTH,), jnp.float32, -3.140625, 3.140625), -3.140625, 3.140625),
    }


def direction_table(length):
    positions = jnp.arange(length, dtype=jnp.int32)
    angles = (positions[:, None] * positions[None, :] % length).astype(jnp.float32) * (2.0 * math.pi / length)
    factor = 1.0 / math.sqrt(length)
    return ((jnp.cos(angles) * factor).astype(jnp.bfloat16), (jnp.sin(angles) * factor).astype(jnp.bfloat16))

def rounded(values):
    return lax.optimization_barrier(values.astype(jnp.bfloat16)).astype(jnp.float32)

def reference(views, phases, kernel_phase):
    table_re, table_im = direction_table(DIRS)
    table_re = table_re.astype(jnp.float32)
    table_im = table_im.astype(jnp.float32)
    angles = phases.astype(jnp.float32) * (2.0 * math.pi / PHASES)
    phase_cos = jnp.cos(angles)
    phase_sin = jnp.sin(angles)
    kernel_turn = jnp.cos(kernel_phase) + 1j * jnp.sin(kernel_phase)
    slabs = jnp.moveaxis(views.reshape(DIRS, HOG_COLS, HROWS, DIRS), 2, 0)

    def one_row(slab_views):
        amplitude = slab_views.astype(jnp.float32)
        wave_re = rounded(amplitude * phase_cos[:, None, :])
        wave_im = rounded(amplitude * phase_sin[:, None, :])
        part_re = jnp.einsum('ucv,vq->ucq', wave_re, table_re) - jnp.einsum('ucv,vq->ucq', wave_im, table_im)
        part_im = jnp.einsum('ucv,vq->ucq', wave_re, table_im) + jnp.einsum('ucv,vq->ucq', wave_im, table_re)
        part_re = rounded(part_re)
        part_im = rounded(part_im)
        field_re = jnp.einsum('up,ucq->pcq', table_re, part_re) - jnp.einsum('up,ucq->pcq', table_im, part_im)
        field_im = jnp.einsum('up,ucq->pcq', table_re, part_im) + jnp.einsum('up,ucq->pcq', table_im, part_re)
        field_re = rounded(field_re).reshape(DIRS, WIDTH)
        field_im = rounded(field_im).reshape(DIRS, WIDTH)
        row_field = field_re + 1j * field_im
        spectrum = jnp.fft.fft(row_field, axis=1) / math.sqrt(WIDTH)
        result = spectrum * kernel_turn[None, :]
        return (jnp.real(result).astype(jnp.float32), jnp.imag(result).astype(jnp.float32))
    out_re, out_im = lax.map(one_row, slabs)
    return (out_re.reshape(ROWS, WIDTH), out_im.reshape(ROWS, WIDTH))
```

```python
import functools
import math

import jax
import jax.numpy as jnp
import numpy as np
from jax import lax
from jax.experimental import pallas as pl
from jax.experimental.pallas import tpu as pltpu
from jax.sharding import Mesh
from jax.sharding import PartitionSpec as P

PHASES = 256
DIRS = 64
SIDE = 256
VIEW = ("xh", "co")
COL = ("y", "zh", "zl", "xl")
HOGEL_GROUP = ("xh", "co", "y", "zh")
SQUARE = ("zl", "xl")
VMEM_BYTES = 40 * 1024 * 1024


def direction_table(length):
    positions = jnp.arange(length, dtype=jnp.int32)
    angles = (positions[:, None] * positions[None, :] % length).astype(jnp.float32) * (
        2.0 * math.pi / length
    )
    factor = 1.0 / math.sqrt(length)
    return (
        (jnp.cos(angles) * factor).astype(jnp.bfloat16),
        (jnp.sin(angles) * factor).astype(jnp.bfloat16),
    )


def numpy_turns(first, second, modulus):
    angles = (np.outer(first, second) % modulus) * (2.0 * np.pi / modulus)
    return np.cos(angles), np.sin(angles)


def params(steps):
    return pltpu.CompilerParams(
        dimension_semantics=("arbitrary",) * steps, vmem_limit_bytes=VMEM_BYTES
    )


def regroup_kernel(views_ref, out_ref, wide_ref):
    dirs, cols, lanes = views_ref.shape
    low_half = lax.broadcasted_iota(jnp.int32, (dirs, 128), 1) < 64
    for pair in range(lanes // 128):
        block = views_ref[:, :, 128 * pair : 128 * (pair + 1)].astype(jnp.float32)
        wide_ref[pair] = block.reshape(dirs * cols, 128)
        for col in range(0, cols, 2):
            even = wide_ref[pair, pl.ds(col, dirs, stride=cols), :]
            odd = wide_ref[pair, pl.ds(col + 1, dirs, stride=cols), :]
            first = jnp.where(low_half, even, pltpu.roll(odd, 64, 1))
            second = jnp.where(low_half, pltpu.roll(even, 64, 1), odd)
            place = slice(64 * col, 64 * col + 128)
            out_ref[2 * pair, :, place] = first.astype(jnp.bfloat16)
            out_ref[2 * pair + 1, :, place] = second.astype(jnp.bfloat16)


def regroup(views, steps=4):
    dirs, cols, merged = views.shape
    lanes = merged // steps
    return pl.pallas_call(
        regroup_kernel,
        grid=(steps,),
        in_specs=[pl.BlockSpec((dirs, cols, lanes), lambda i: (0, 0, i))],
        out_specs=pl.BlockSpec((lanes // 64, dirs, cols * 64), lambda i: (i, 0, 0)),
        out_shape=jax.ShapeDtypeStruct((merged // 64, dirs, cols * 64), jnp.bfloat16),
        scratch_shapes=[pltpu.VMEM((lanes // 128, dirs * cols, 128), jnp.float32)],
        compiler_params=params(1),
        name="regroup",
    )(views)


def field_kernel(rays_ref, cos_ref, sin_ref, inner_ref, outer_ref, *rest):
    out_refs, wave_ref, wide_ref = rest[:4], rest[4], rest[5]
    rays = rays_ref[...].reshape(DIRS, 32 * DIRS)
    phase_cos = cos_ref[...]
    phase_sin = sin_ref[...]
    for tile in range(16):
        amplitude = rays[:, 128 * tile : 128 * (tile + 1)].astype(jnp.float32)
        rows = slice(DIRS * tile, DIRS * (tile + 1))
        wave_ref[rows, 0:128] = (amplitude * phase_cos).astype(jnp.bfloat16)
        wave_ref[rows, 128:256] = (amplitude * phase_sin).astype(jnp.bfloat16)
    inner = inner_ref[...]
    outer = outer_ref[...]
    for half in range(8):
        rows = slice(2 * DIRS * half, 2 * DIRS * (half + 1))
        part = jnp.dot(wave_ref[rows, :], inner, preferred_element_type=jnp.float32)
        part = part.astype(jnp.bfloat16)
        left = jnp.concatenate([part[:DIRS, :128], part[:DIRS, 128:]], axis=0)
        right = jnp.concatenate([part[DIRS:, :128], part[DIRS:, 128:]], axis=0)
        stacked = jnp.concatenate([left, right], axis=1)
        field = jnp.dot(outer, stacked, preferred_element_type=jnp.float32)
        wide_ref[0, pl.ds(half, DIRS, stride=16), :] = field[:DIRS, :128]
        wide_ref[1, pl.ds(half, DIRS, stride=16), :] = field[:DIRS, 128:]
        wide_ref[0, pl.ds(8 + half, DIRS, stride=16), :] = field[DIRS:, :128]
        wide_ref[1, pl.ds(8 + half, DIRS, stride=16), :] = field[DIRS:, 128:]
    for quarter in range(4):
        rows = slice(256 * quarter, 256 * (quarter + 1))
        for side in range(2):
            out_refs[quarter][0, :, :, 128 * side : 128 * (side + 1)] = (
                wide_ref[side, rows, :].astype(jnp.bfloat16).reshape(16, 16, 128)
            )


def fields(rays, phase_cos, phase_sin, inner, outer):
    groups = rays.shape[1]
    whole = lambda i: (0, 0)
    return pl.pallas_call(
        field_kernel,
        grid=(groups,),
        in_specs=[
            pl.BlockSpec((4, 1, 16, 2048), lambda i: (0, i, 0, 0)),
            pl.BlockSpec((DIRS, 128), whole),
            pl.BlockSpec((DIRS, 128), whole),
            pl.BlockSpec((256, 256), whole),
            pl.BlockSpec((128, 128), whole),
        ],
        out_specs=[pl.BlockSpec((1, 16, 16, 256), lambda i: (i, 0, 0, 0))] * 4,
        out_shape=[jax.ShapeDtypeStruct((groups, 16, 16, 256), jnp.bfloat16)] * 4,
        scratch_shapes=[
            pltpu.VMEM((1024, 256), jnp.bfloat16),
            pltpu.VMEM((2, 1024, 128), jnp.float32),
        ],
        compiler_params=params(1),
        name="fields",
    )(rays, phase_cos, phase_sin, inner, outer)


def spectrum_kernel(*refs):
    pieces = refs[:4]
    first_ref, twist_re_ref, twist_im_ref, second_ref, turn_re_ref, turn_im_ref = refs[4:10]
    re_ref, im_ref = refs[10:]
    row = pl.program_id(0) % 8
    signal = jnp.concatenate([p[...].reshape(128, SIDE) for p in pieces], axis=0)
    section = jnp.dot(first_ref[...], signal, preferred_element_type=jnp.float32)
    section_re, section_im = section[:SIDE], section[SIDE:]
    twist_re, twist_im = twist_re_ref[...], twist_im_ref[...]
    turned_re = (section_re * twist_re - section_im * twist_im).astype(jnp.bfloat16)
    turned_im = (section_re * twist_im + section_im * twist_re).astype(jnp.bfloat16)
    turned = jnp.concatenate([turned_re, turned_im], axis=1)
    final = lax.dot_general(
        second_ref[...],
        turned,
        (((1,), (1,)), ((), ())),
        preferred_element_type=jnp.float32,
    )
    final_re, final_im = final[:SIDE], final[SIDE:]
    turn_re, turn_im = turn_re_ref[...], turn_im_ref[...]
    out_re = final_re * turn_re - final_im * turn_im
    out_im = final_re * turn_im + final_im * turn_re
    for side in range(2):
        lanes = slice(128 * side, 128 * (side + 1))
        rows = pl.ds(8 * side + row, SIDE, stride=16)
        re_ref[rows, :] = out_re[:, lanes]
        im_ref[rows, :] = out_im[:, lanes]


def spectra(pieces, first, twist_re, twist_im, second, turn_re, turn_im):
    groups, rows = pieces[0].shape[:2]
    whole = lambda i: (0, 0)
    piece = pl.BlockSpec((groups, 1, 16, SIDE), lambda i: (0, i, 0, 0))
    square = pl.BlockSpec((SIDE, SIDE), whole)
    big = pl.BlockSpec((2 * SIDE, 2 * SIDE), whole)
    out_block = pl.BlockSpec((16 * SIDE, 128), lambda i: (i // 8, 0))
    out_shape = jax.ShapeDtypeStruct((rows // 8 * 16 * SIDE, 128), jnp.float32)
    return pl.pallas_call(
        spectrum_kernel,
        grid=(rows,),
        in_specs=[piece] * 4 + [big, square, square, big, square, square],
        out_specs=[out_block, out_block],
        out_shape=[out_shape, out_shape],
        compiler_params=params(1),
        name="spectra",
    )(*pieces, first, twist_re, twist_im, second, turn_re, turn_im)


def inner_outer_tables():
    table_re, table_im = direction_table(DIRS)
    zero = jnp.zeros_like(table_re)
    twice = lambda t: jnp.block([[t, zero], [zero, t]])
    inner = jnp.block(
        [[twice(table_re), twice(table_im)], [twice(-table_im), twice(table_re)]]
    )
    outer = jnp.block([[table_re, -table_im], [table_im, table_re]])
    return inner, outer


def first_tables():
    source = np.arange(4)[:, None, None]
    group = np.arange(8)[None, :, None]
    low = np.arange(8)[None, None, :]
    places = 32 * group + 8 * source + low
    cosine, sine = numpy_turns(np.arange(SIDE), places.reshape(-1), SIDE)
    shape = (SIDE, 4, 8, 8)
    cosine = cosine.reshape(shape) / 16.0
    sine = sine.reshape(shape) / 16.0
    upper = np.stack([cosine, sine], axis=3)
    lower = np.stack([-sine, cosine], axis=3)
    table = np.concatenate([upper, lower], axis=0).reshape(2 * SIDE, 4, 128)
    return jnp.asarray(table.transpose(1, 0, 2), dtype=jnp.bfloat16)


def second_table():
    cosine, sine = numpy_turns(np.arange(SIDE), np.arange(SIDE), SIDE)
    table = np.block([[cosine, sine], [-sine, cosine]]) / 16.0
    return jnp.asarray(table, dtype=jnp.bfloat16)


def twist_tables():
    cosine, sine = numpy_turns(np.arange(SIDE), np.arange(SIDE), SIDE * SIDE)
    return jnp.asarray(cosine, dtype=jnp.float32), jnp.asarray(-sine, dtype=jnp.float32)


def to_rows(flat):
    rows = flat.shape[0] // (16 * SIDE) * 8
    tiles = flat.reshape(rows // 8, SIDE, 2, 8, 128)
    return tiles.transpose(0, 3, 1, 2, 4).reshape(rows, SIDE * SIDE)


def per_device(views, phases, kernel_phase):
    sent = regroup(views)
    rays = lax.all_to_all(sent, HOGEL_GROUP, split_axis=0, concat_axis=0, tiled=True)
    angles = phases.astype(jnp.float32) * (2.0 * math.pi / PHASES)
    phase_cos = jnp.tile(jnp.cos(angles), (1, 2))
    phase_sin = jnp.tile(jnp.sin(angles), (1, 2))
    inner, outer = inner_outer_tables()
    quarters = fields(rays.reshape(4, 8, 16, 2048), phase_cos, phase_sin, inner, outer)
    me = lax.axis_index("zl") * 2 + lax.axis_index("xl")
    stacked = jnp.stack(quarters)
    got = lax.all_to_all(stacked, SQUARE, split_axis=0, concat_axis=0, tiled=True)
    pieces = [got[d] for d in range(4)]
    first = first_tables().transpose(1, 0, 2).reshape(2 * SIDE, 2 * SIDE)
    twist_re, twist_im = twist_tables()
    turn = kernel_phase.reshape(SIDE, SIDE)
    flat_re, flat_im = spectra(
        pieces, first, twist_re, twist_im, second_table(), jnp.cos(turn), jnp.sin(turn)
    )
    return to_rows(flat_re), to_rows(flat_im)


def solution(mesh):
    fine = Mesh(mesh.devices.reshape(2, 2, 4, 2, 2, 2), VIEW + COL)
    in_specs = (P(VIEW, COL, None), P(), P())
    out_specs = (P(VIEW + COL, None), P(VIEW + COL, None))
    return jax.shard_map(
        per_device, mesh=fine, in_specs=in_specs, out_specs=out_specs, check_vma=False
    )
```

```python
import functools
import math

import jax
import jax.numpy as jnp
import numpy as np
from jax import lax
from jax.experimental import pallas as pl
from jax.experimental.pallas import tpu as pltpu
from jax.sharding import Mesh
from jax.sharding import PartitionSpec as P

PHASES = 256
DIRS = 64
SIDE = 256
VIEW = ("xh", "co")
COL = ("y", "zh", "zl", "xl")
HOGEL_GROUP = ("xh", "co", "y", "zh")
SQUARE = ("zl", "xl")
VMEM_BYTES = 40 * 1024 * 1024


def direction_table(length):
    positions = jnp.arange(length, dtype=jnp.int32)
    angles = (positions[:, None] * positions[None, :] % length).astype(jnp.float32) * (
        2.0 * math.pi / length
    )
    factor = 1.0 / math.sqrt(length)
    return (
        (jnp.cos(angles) * factor).astype(jnp.bfloat16),
        (jnp.sin(angles) * factor).astype(jnp.bfloat16),
    )


def numpy_turns(first, second, modulus):
    angles = (np.outer(first, second) % modulus) * (2.0 * np.pi / modulus)
    return np.cos(angles), np.sin(angles)


def params(steps):
    return pltpu.CompilerParams(
        dimension_semantics=("arbitrary",) * steps, vmem_limit_bytes=VMEM_BYTES
    )


def regroup_kernel(views_ref, out_ref, wide_ref):
    dirs, cols, lanes = views_ref.shape
    low_half = lax.broadcasted_iota(jnp.int32, (dirs, 128), 1) < 64
    for pair in range(lanes // 128):
        block = views_ref[:, :, 128 * pair : 128 * (pair + 1)].astype(jnp.float32)
        wide_ref[pair] = block.reshape(dirs * cols, 128)
        for col in range(0, cols, 2):
            even = wide_ref[pair, pl.ds(col, dirs, stride=cols), :]
            odd = wide_ref[pair, pl.ds(col + 1, dirs, stride=cols), :]
            first = jnp.where(low_half, even, pltpu.roll(odd, 64, 1))
            second = jnp.where(low_half, pltpu.roll(even, 64, 1), odd)
            place = slice(64 * col, 64 * col + 128)
            out_ref[2 * pair, :, place] = first.astype(jnp.bfloat16)
            out_ref[2 * pair + 1, :, place] = second.astype(jnp.bfloat16)


def regroup(views, steps=4):
    dirs, cols, merged = views.shape
    lanes = merged // steps
    return pl.pallas_call(
        regroup_kernel,
        grid=(steps,),
        in_specs=[pl.BlockSpec((dirs, cols, lanes), lambda i: (0, 0, i))],
        out_specs=pl.BlockSpec((lanes // 64, dirs, cols * 64), lambda i: (i, 0, 0)),
        out_shape=jax.ShapeDtypeStruct((merged // 64, dirs, cols * 64), jnp.bfloat16),
        scratch_shapes=[pltpu.VMEM((lanes // 128, dirs * cols, 128), jnp.float32)],
        compiler_params=params(1),
        name="regroup",
    )(views)


def field_kernel(rays_ref, cos_ref, sin_ref, inner_ref, outer_ref, *rest):
    out_refs, wave_ref, wide_ref = rest[:4], rest[4], rest[5]
    rays = rays_ref[...].reshape(DIRS, 32 * DIRS)
    phase_cos = cos_ref[...]
    phase_sin = sin_ref[...]
    for tile in range(16):
        amplitude = rays[:, 128 * tile : 128 * (tile + 1)].astype(jnp.float32)
        rows = slice(DIRS * tile, DIRS * (tile + 1))
        wave_ref[rows, 0:128] = (amplitude * phase_cos).astype(jnp.bfloat16)
        wave_ref[rows, 128:256] = (amplitude * phase_sin).astype(jnp.bfloat16)
    inner = inner_ref[...]
    outer = outer_ref[...]
    count = outer.shape[0] // 2
    for low in range(8):
        rows = slice(2 * DIRS * low, 2 * DIRS * (low + 1))
        part = jnp.dot(wave_ref[rows, :], inner, preferred_element_type=jnp.float32)
        part = part.astype(jnp.bfloat16)
        left = jnp.concatenate([part[:DIRS, :128], part[:DIRS, 128:]], axis=0)
        right = jnp.concatenate([part[DIRS:, :128], part[DIRS:, 128:]], axis=0)
        stacked = jnp.concatenate([left, right], axis=1)
        field = jnp.dot(outer, stacked, preferred_element_type=jnp.float32)
        for side in range(2):
            lanes = slice(128 * side, 128 * (side + 1))
            wide_ref[side, pl.ds(low, count, stride=16), :] = field[:count, lanes]
            wide_ref[side, pl.ds(8 + low, count, stride=16), :] = field[count:, lanes]
    each = count // 4
    for partner in range(4):
        rows = slice(16 * each * partner, 16 * each * (partner + 1))
        for side in range(2):
            out_refs[partner][0, :, :, 128 * side : 128 * (side + 1)] = (
                wide_ref[side, rows, :].astype(jnp.bfloat16).reshape(each, 16, 128)
            )


def fields(rays, phase_cos, phase_sin, inner, outer):
    groups = rays.shape[1]
    count = outer.shape[0] // 2
    whole = lambda i: (0, 0)
    return pl.pallas_call(
        field_kernel,
        grid=(groups,),
        in_specs=[
            pl.BlockSpec((4, 1, 16, 2048), lambda i: (0, i, 0, 0)),
            pl.BlockSpec((DIRS, 128), whole),
            pl.BlockSpec((DIRS, 128), whole),
            pl.BlockSpec((256, 256), whole),
            pl.BlockSpec((2 * count, 128), whole),
        ],
        out_specs=[pl.BlockSpec((1, count // 4, 16, 256), lambda i: (i, 0, 0, 0))] * 4,
        out_shape=[jax.ShapeDtypeStruct((groups, count // 4, 16, 256), jnp.bfloat16)] * 4,
        scratch_shapes=[
            pltpu.VMEM((1024, 256), jnp.bfloat16),
            pltpu.VMEM((2, 16 * count, 128), jnp.float32),
        ],
        compiler_params=params(1),
        cost_estimate=pl.CostEstimate(
            flops=2 * 10**9, bytes_accessed=4 * 2**20, transcendentals=0
        ),
        name="fields",
    )(rays, phase_cos, phase_sin, inner, outer)


def spectrum_kernel(filled, *refs):
    pieces = refs[:4]
    first_ref, twist_re_ref, twist_im_ref, second_ref, turn_re_ref, turn_im_ref = refs[4:10]
    re_ref, im_ref = refs[10 + filled :]
    row = pl.program_id(0)
    signal = jnp.concatenate([p[...].reshape(128, SIDE) for p in pieces], axis=0)
    section = jnp.dot(first_ref[...], signal, preferred_element_type=jnp.float32)
    section_re, section_im = section[:SIDE], section[SIDE:]
    twist_re, twist_im = twist_re_ref[...], twist_im_ref[...]
    turned_re = (section_re * twist_re - section_im * twist_im).astype(jnp.bfloat16)
    turned_im = (section_re * twist_im + section_im * twist_re).astype(jnp.bfloat16)
    turned = jnp.concatenate([turned_re, turned_im], axis=1)
    final = lax.dot_general(
        second_ref[...],
        turned,
        (((1,), (1,)), ((), ())),
        preferred_element_type=jnp.float32,
    )
    final_re, final_im = final[:SIDE], final[SIDE:]
    turn_re, turn_im = turn_re_ref[...], turn_im_ref[...]
    out_re = final_re * turn_re - final_im * turn_im
    out_im = final_re * turn_im + final_im * turn_re
    for side in range(2):
        lanes = slice(128 * side, 128 * (side + 1))
        rows = pl.ds(8 * side + row, SIDE, stride=16)
        re_ref[rows, :] = out_re[:, lanes]
        im_ref[rows, :] = out_im[:, lanes]


def spectra(pieces, tables, half, filled):
    groups, rows = pieces[0].shape[:2]
    whole = lambda i: (0, 0)
    piece = pl.BlockSpec((groups, 1, 16, SIDE), lambda i: (0, i, 0, 0))
    square = pl.BlockSpec((SIDE, SIDE), whole)
    big = pl.BlockSpec((2 * SIDE, 2 * SIDE), whole)
    out_block = pl.BlockSpec((16 * SIDE, 128), lambda i: (half, 0))
    out_shape = jax.ShapeDtypeStruct((2 * 16 * SIDE, 128), jnp.float32)
    aliases = {10 + i: i for i in range(len(filled))}
    return pl.pallas_call(
        functools.partial(spectrum_kernel, len(filled)),
        grid=(rows,),
        in_specs=[piece] * 4
        + [big, square, square, big, square, square]
        + [pl.BlockSpec(memory_space=pl.ANY)] * len(filled),
        out_specs=[out_block, out_block],
        out_shape=[out_shape, out_shape],
        input_output_aliases=aliases,
        compiler_params=params(1),
        cost_estimate=pl.CostEstimate(
            flops=8 * 10**9, bytes_accessed=8 * 2**20, transcendentals=0
        ),
        name="spectra",
    )(*pieces, *tables, *filled)


def inner_outer_tables():
    table_re, table_im = direction_table(DIRS)
    zero = jnp.zeros_like(table_re)
    twice = lambda t: jnp.block([[t, zero], [zero, t]])
    inner = jnp.block(
        [[twice(table_re), twice(table_im)], [twice(-table_im), twice(table_re)]]
    )
    outer = jnp.stack(
        [
            jnp.concatenate([table_re, -table_im], axis=1),
            jnp.concatenate([table_im, table_re], axis=1),
        ]
    )
    return inner, outer.reshape(2, 4, 2, 8, 2 * DIRS)


def first_tables():
    source = np.arange(4)[:, None, None]
    group = np.arange(8)[None, :, None]
    low = np.arange(8)[None, None, :]
    places = 32 * group + 8 * source + low
    cosine, sine = numpy_turns(np.arange(SIDE), places.reshape(-1), SIDE)
    shape = (SIDE, 4, 8, 8)
    cosine = cosine.reshape(shape) / 16.0
    sine = sine.reshape(shape) / 16.0
    upper = np.stack([cosine, sine], axis=3)
    lower = np.stack([-sine, cosine], axis=3)
    table = np.concatenate([upper, lower], axis=0).reshape(2 * SIDE, 4, 128)
    return jnp.asarray(table.transpose(1, 0, 2), dtype=jnp.bfloat16)


def second_table():
    cosine, sine = numpy_turns(np.arange(SIDE), np.arange(SIDE), SIDE)
    table = np.block([[cosine, sine], [-sine, cosine]]) / 16.0
    return jnp.asarray(table, dtype=jnp.bfloat16)


def twist_tables():
    cosine, sine = numpy_turns(np.arange(SIDE), np.arange(SIDE), SIDE * SIDE)
    return jnp.asarray(cosine, dtype=jnp.float32), jnp.asarray(-sine, dtype=jnp.float32)


def to_rows(flat):
    rows = flat.shape[0] // (16 * SIDE) * 8
    tiles = flat.reshape(rows // 8, SIDE, 2, 8, 128)
    return tiles.transpose(0, 3, 1, 2, 4).reshape(rows, SIDE * SIDE)


def per_device(views, phases, kernel_phase):
    sent = regroup(views)
    rays = lax.all_to_all(sent, HOGEL_GROUP, split_axis=0, concat_axis=0, tiled=True)
    rays = rays.reshape(4, 8, 16, 2048)
    angles = phases.astype(jnp.float32) * (2.0 * math.pi / PHASES)
    phase_cos = jnp.tile(jnp.cos(angles), (1, 2))
    phase_sin = jnp.tile(jnp.sin(angles), (1, 2))
    inner, outer = inner_outer_tables()
    me = lax.axis_index("zl") * 2 + lax.axis_index("xl")
    partners = [me ^ d for d in range(4)]
    pick = lambda table, at, axis: lax.dynamic_index_in_dim(table, at, axis, False)
    outer = jnp.stack([pick(outer, at, 1) for at in partners], axis=1)
    source_tables = first_tables()
    first = jnp.concatenate([pick(source_tables, at, 0) for at in partners], axis=1)
    twist_re, twist_im = twist_tables()
    turn = kernel_phase.reshape(SIDE, SIDE)
    tables = (first, twist_re, twist_im, second_table(), jnp.cos(turn), jnp.sin(turn))
    halves = []
    for half in range(2):
        outer_half = outer[:, :, half].reshape(2 * 4 * 8, 2 * DIRS)
        sending = fields(rays, phase_cos, phase_sin, inner, outer_half)
        pieces = [sending[0], None, None, None]
        for d in (3, 1, 2):
            swaps = [(i, i ^ d) for i in range(4)]
            pieces[d] = lax.ppermute(sending[d], SQUARE, swaps)
        halves.append(pieces)
    filled = spectra(halves[0], tables, 0, ())
    flat_re, flat_im = spectra(halves[1], tables, 1, filled)
    return to_rows(flat_re), to_rows(flat_im)


def solution(mesh):
    fine = Mesh(mesh.devices.reshape(2, 2, 4, 2, 2, 2), VIEW + COL)
    in_specs = (P(VIEW, COL, None), P(), P())
    out_specs = (P(VIEW + COL, None), P(VIEW + COL, None))
    return jax.shard_map(
        per_device, mesh=fine, in_specs=in_specs, out_specs=out_specs, check_vma=False
    )
```

```python
import functools
import math

import jax
import jax.numpy as jnp
import numpy as np
from jax import lax
from jax.experimental import pallas as pl
from jax.experimental.pallas import tpu as pltpu
from jax.sharding import Mesh
from jax.sharding import PartitionSpec as P

PHASES = 256
DIRS = 64
SIDE = 256
VIEW = ("xh", "co")
COL = ("y", "zh", "zl", "xl")
HOGEL_GROUP = ("xh", "co", "y", "zh")
SQUARE = ("zl", "xl")
VMEM_BYTES = 40 * 1024 * 1024


def direction_table(length):
    positions = jnp.arange(length, dtype=jnp.int32)
    angles = (positions[:, None] * positions[None, :] % length).astype(jnp.float32) * (
        2.0 * math.pi / length
    )
    factor = 1.0 / math.sqrt(length)
    return (
        (jnp.cos(angles) * factor).astype(jnp.bfloat16),
        (jnp.sin(angles) * factor).astype(jnp.bfloat16),
    )


def numpy_turns(first, second, modulus):
    angles = (np.outer(first, second) % modulus) * (2.0 * np.pi / modulus)
    return np.cos(angles), np.sin(angles)


def params(limit=VMEM_BYTES):
    return pltpu.CompilerParams(
        dimension_semantics=("arbitrary",), vmem_limit_bytes=limit
    )


def regroup_kernel(views_ref, out_ref):
    dirs, cols, lanes = views_ref.shape
    low_half = lax.broadcasted_iota(jnp.int32, (dirs, 128), 1) < 64
    for pair in range(lanes // 128):
        block = views_ref[:, :, 128 * pair : 128 * (pair + 1)]
        block = jnp.swapaxes(block, 0, 1).astype(jnp.float32)
        for col in range(0, cols, 2):
            even, odd = block[col], block[col + 1]
            first = jnp.where(low_half, even, pltpu.roll(odd, 64, 1))
            second = jnp.where(low_half, pltpu.roll(even, 64, 1), odd)
            place = slice(64 * col, 64 * col + 128)
            out_ref[2 * pair, :, place] = first.astype(jnp.bfloat16)
            out_ref[2 * pair + 1, :, place] = second.astype(jnp.bfloat16)


def regroup(views, steps=2):
    dirs, cols, merged = views.shape
    lanes = merged // steps
    return pl.pallas_call(
        regroup_kernel,
        grid=(steps,),
        in_specs=[pl.BlockSpec((dirs, cols, lanes), lambda i: (0, 0, i))],
        out_specs=pl.BlockSpec((lanes // 64, dirs, cols * 64), lambda i: (i, 0, 0)),
        out_shape=jax.ShapeDtypeStruct((merged // 64, dirs, cols * 64), jnp.bfloat16),
        compiler_params=params(60 * 1024 * 1024),
        name="regroup",
    )(views)


def field_kernel(rays_ref, cos_ref, sin_ref, inner_ref, outer_ref, *out_refs):
    phase_cos = cos_ref[...]
    phase_sin = sin_ref[...]
    inner = inner_ref[...]
    outer = outer_ref[...]
    count = outer.shape[0] // 2
    each = count // 4
    groups = rays_ref.shape[1]
    stacked = []
    for group in range(groups):
        rays = rays_ref[:, group].reshape(DIRS, 32 * DIRS)

        def wave(tile):
            amplitude = rays[:, 128 * tile : 128 * (tile + 1)].astype(jnp.float32)
            wave_re = (amplitude * phase_cos).astype(jnp.bfloat16)
            wave_im = (amplitude * phase_sin).astype(jnp.bfloat16)
            return jnp.concatenate([wave_re, wave_im], axis=1)

        parts = []
        for low in range(8):
            waves = jnp.concatenate([wave(2 * low), wave(2 * low + 1)], axis=0)
            part = jnp.dot(waves, inner, preferred_element_type=jnp.float32)
            parts.append(part.astype(jnp.bfloat16))
        for part in parts:
            left = jnp.concatenate([part[:DIRS, :128], part[:DIRS, 128:]], axis=0)
            right = jnp.concatenate([part[DIRS:, :128], part[DIRS:, 128:]], axis=0)
            stacked.append(jnp.concatenate([left, right], axis=1))
    field = [jnp.dot(outer, s, preferred_element_type=jnp.float32) for s in stacked]
    for group in range(groups):
        own = field[8 * group : 8 * (group + 1)]
        sides = []
        for rows in (slice(0, count), slice(count, 2 * count)):
            sides.append(jnp.swapaxes(jnp.stack([f[rows] for f in own]), 0, 1))
        block = jnp.concatenate(sides, axis=1).astype(jnp.bfloat16)
        for partner in range(4):
            out_refs[partner][group] = block[each * partner : each * (partner + 1)]


def fields(rays, phase_cos, phase_sin, inner, outer, step=2):
    groups = rays.shape[1]
    count = outer.shape[0] // 2
    whole = lambda i: (0, 0)
    out_block = pl.BlockSpec((step, count // 4, 16, 256), lambda i: (i, 0, 0, 0))
    return pl.pallas_call(
        field_kernel,
        grid=(groups // step,),
        in_specs=[
            pl.BlockSpec((4, step, 16, 2048), lambda i: (0, i, 0, 0)),
            pl.BlockSpec((DIRS, 128), whole),
            pl.BlockSpec((DIRS, 128), whole),
            pl.BlockSpec((256, 256), whole),
            pl.BlockSpec((2 * count, 128), whole),
        ],
        out_specs=[out_block] * 4,
        out_shape=[jax.ShapeDtypeStruct((groups, count // 4, 16, 256), jnp.bfloat16)] * 4,
        compiler_params=params(),
        cost_estimate=pl.CostEstimate(
            flops=2 * 10**9, bytes_accessed=4 * 2**20, transcendentals=0
        ),
        name="fields",
    )(rays, phase_cos, phase_sin, inner, outer)


def spectrum_kernel(filled, *refs):
    pieces = refs[:4]
    first_ref, twist_re_ref, twist_im_ref, second_ref, turn_re_ref, turn_im_ref = refs[4:10]
    re_ref, im_ref, turned_ref = refs[10 + filled :]
    rows = turned_ref.shape[0]

    @pl.when(pl.program_id(0) == 0)
    def _():
        for row in range(rows):
            signal = [p[:, row].reshape(128, SIDE) for p in pieces]
            signal = jnp.concatenate(signal, axis=0)
            section = jnp.dot(first_ref[...], signal, preferred_element_type=jnp.float32)
            section_re, section_im = section[:SIDE], section[SIDE:]
            twist_re, twist_im = twist_re_ref[...], twist_im_ref[...]
            turned_re = section_re * twist_re - section_im * twist_im
            turned_im = section_re * twist_im + section_im * twist_re
            turned_ref[row, :, :SIDE] = turned_re.astype(jnp.bfloat16)
            turned_ref[row, :, SIDE:] = turned_im.astype(jnp.bfloat16)

    half = SIDE // 2
    second = second_ref[...].reshape(2 * half, 2 * SIDE)
    for row in range(rows):
        final = lax.dot_general(
            second,
            turned_ref[row],
            (((1,), (1,)), ((), ())),
            preferred_element_type=jnp.float32,
        )
        final_re, final_im = final[:half], final[half:]
        turn_re, turn_im = turn_re_ref[...], turn_im_ref[...]
        out_re = final_re * turn_re - final_im * turn_im
        out_im = final_re * turn_im + final_im * turn_re
        for side in range(2):
            lanes = slice(128 * side, 128 * (side + 1))
            place = pl.ds(8 * side + row, half, stride=16)
            re_ref[place, :] = out_re[:, lanes]
            im_ref[place, :] = out_im[:, lanes]


def spectra(pieces, tables, half, filled):
    groups, rows = pieces[0].shape[:2]
    whole = lambda i: (0, 0)
    piece = pl.BlockSpec((groups, rows, 16, SIDE), lambda i: (0, 0, 0, 0))
    square = pl.BlockSpec((SIDE, SIDE), whole)
    first = pl.BlockSpec((2 * SIDE, 2 * SIDE), whole)
    second = pl.BlockSpec((2, SIDE // 2, 2 * SIDE), lambda i: (0, i, 0))
    turn = pl.BlockSpec((SIDE // 2, SIDE), lambda i: (i, 0))
    out_block = pl.BlockSpec((8 * SIDE, 128), lambda i: (2 * half + i, 0))
    out_shape = jax.ShapeDtypeStruct((2 * 16 * SIDE, 128), jnp.float32)
    aliases = {10 + i: i for i in range(len(filled))}
    return pl.pallas_call(
        functools.partial(spectrum_kernel, len(filled)),
        grid=(2,),
        in_specs=[piece] * 4
        + [first, square, square, second, turn, turn]
        + [pl.BlockSpec(memory_space=pl.ANY)] * len(filled),
        out_specs=[out_block, out_block],
        out_shape=[out_shape, out_shape],
        scratch_shapes=[pltpu.VMEM((rows, SIDE, 2 * SIDE), jnp.bfloat16)],
        input_output_aliases=aliases,
        compiler_params=params(),
        cost_estimate=pl.CostEstimate(
            flops=8 * 10**9, bytes_accessed=8 * 2**20, transcendentals=0
        ),
        name="spectra",
    )(*pieces, *tables, *filled)


def inner_outer_tables():
    table_re, table_im = direction_table(DIRS)
    zero = jnp.zeros_like(table_re)
    twice = lambda t: jnp.block([[t, zero], [zero, t]])
    inner = jnp.block(
        [[twice(table_re), twice(table_im)], [twice(-table_im), twice(table_re)]]
    )
    outer = jnp.stack(
        [
            jnp.concatenate([table_re, -table_im], axis=1),
            jnp.concatenate([table_im, table_re], axis=1),
        ]
    )
    return inner, outer.reshape(2, 4, 2, 8, 2 * DIRS)


def first_tables():
    source = np.arange(4)[:, None, None]
    group = np.arange(8)[None, :, None]
    low = np.arange(8)[None, None, :]
    places = 32 * group + 8 * source + low
    cosine, sine = numpy_turns(np.arange(SIDE), places.reshape(-1), SIDE)
    shape = (SIDE, 4, 8, 8)
    cosine = cosine.reshape(shape) / 16.0
    sine = sine.reshape(shape) / 16.0
    upper = np.stack([cosine, sine], axis=3)
    lower = np.stack([-sine, cosine], axis=3)
    table = np.concatenate([upper, lower], axis=0).reshape(2 * SIDE, 4, 128)
    return jnp.asarray(table.transpose(1, 0, 2), dtype=jnp.bfloat16)


def second_table():
    cosine, sine = numpy_turns(np.arange(SIDE), np.arange(SIDE), SIDE)
    table = np.block([[cosine, sine], [-sine, cosine]]) / 16.0
    return jnp.asarray(table.reshape(2, SIDE, 2 * SIDE), dtype=jnp.bfloat16)


def twist_tables():
    cosine, sine = numpy_turns(np.arange(SIDE), np.arange(SIDE), SIDE * SIDE)
    return jnp.asarray(cosine, dtype=jnp.float32), jnp.asarray(-sine, dtype=jnp.float32)


def to_rows(flat):
    rows = flat.shape[0] // (16 * SIDE) * 8
    tiles = flat.reshape(rows // 8, SIDE, 2, 8, 128)
    return tiles.transpose(0, 3, 1, 2, 4).reshape(rows, SIDE * SIDE)


def per_device(views, phases, kernel_phase):
    sent = regroup(views)
    rays = lax.all_to_all(sent, HOGEL_GROUP, split_axis=0, concat_axis=0, tiled=True)
    rays = rays.reshape(4, 8, 16, 2048)
    angles = phases.astype(jnp.float32) * (2.0 * math.pi / PHASES)
    phase_cos = jnp.tile(jnp.cos(angles), (1, 2))
    phase_sin = jnp.tile(jnp.sin(angles), (1, 2))
    inner, outer = inner_outer_tables()
    me = lax.axis_index("zl") * 2 + lax.axis_index("xl")
    partners = [me ^ d for d in range(4)]
    pick = lambda table, at, axis: lax.dynamic_index_in_dim(table, at, axis, False)
    outer = jnp.stack([pick(outer, at, 1) for at in partners], axis=1)
    source_tables = first_tables()
    first = jnp.concatenate([pick(source_tables, at, 0) for at in partners], axis=1)
    twist_re, twist_im = twist_tables()
    turn = kernel_phase.reshape(SIDE, SIDE)
    tables = (first, twist_re, twist_im, second_table(), jnp.cos(turn), jnp.sin(turn))
    halves = []
    for half in range(2):
        outer_half = outer[:, :, half].reshape(2 * 4 * 8, 2 * DIRS)
        sending = fields(rays, phase_cos, phase_sin, inner, outer_half)
        pieces = [sending[0], None, None, None]
        for d in (3, 1, 2):
            swaps = [(i, i ^ d) for i in range(4)]
            pieces[d] = lax.ppermute(sending[d], SQUARE, swaps)
        halves.append(pieces)
    filled = spectra(halves[0], tables, 0, ())
    flat_re, flat_im = spectra(halves[1], tables, 1, filled)
    return to_rows(flat_re), to_rows(flat_im)


def solution(mesh):
    fine = Mesh(mesh.devices.reshape(2, 2, 4, 2, 2, 2), VIEW + COL)
    in_specs = (P(VIEW, COL, None), P(), P())
    out_specs = (P(VIEW + COL, None), P(VIEW + COL, None))
    return jax.shard_map(
        per_device, mesh=fine, in_specs=in_specs, out_specs=out_specs, check_vma=False
    )
```

```python
import functools
import math

import jax
import jax.numpy as jnp
import numpy as np
from jax import lax
from jax.experimental import pallas as pl
from jax.experimental.pallas import tpu as pltpu
from jax.sharding import Mesh
from jax.sharding import PartitionSpec as P

PHASES = 256
DIRS = 64
SIDE = 256
VIEW = ("xh", "co")
COL = ("y", "zh", "zl", "xl")
HOGEL_GROUP = ("xh", "co", "y", "zh")
SQUARE = ("zl", "xl")
VMEM_BYTES = 40 * 1024 * 1024


def direction_table(length):
    positions = jnp.arange(length, dtype=jnp.int32)
    angles = (positions[:, None] * positions[None, :] % length).astype(jnp.float32) * (
        2.0 * math.pi / length
    )
    factor = 1.0 / math.sqrt(length)
    return (
        (jnp.cos(angles) * factor).astype(jnp.bfloat16),
        (jnp.sin(angles) * factor).astype(jnp.bfloat16),
    )


def numpy_turns(first, second, modulus):
    angles = (np.outer(first, second) % modulus) * (2.0 * np.pi / modulus)
    return np.cos(angles), np.sin(angles)


def params(limit=VMEM_BYTES):
    return pltpu.CompilerParams(
        dimension_semantics=("arbitrary",), vmem_limit_bytes=limit
    )


def regroup_kernel(views_ref, out_ref):
    dirs, cols, lanes = views_ref.shape
    for pair in range(lanes // 128):
        block = jnp.swapaxes(views_ref[:, :, 128 * pair : 128 * (pair + 1)], 0, 1)
        for col in range(0, cols, 2):
            even, odd = block[col], block[col + 1]
            place = slice(64 * col, 64 * col + 128)
            for side in range(2):
                own = slice(64 * side, 64 * (side + 1))
                joined = jnp.concatenate([even[:, own], odd[:, own]], axis=1)
                out_ref[2 * pair + side, :, place] = joined


def regroup(views, steps=2):
    dirs, cols, merged = views.shape
    lanes = merged // steps
    return pl.pallas_call(
        regroup_kernel,
        grid=(steps,),
        in_specs=[pl.BlockSpec((dirs, cols, lanes), lambda i: (0, 0, i))],
        out_specs=pl.BlockSpec((lanes // 64, dirs, cols * 64), lambda i: (i, 0, 0)),
        out_shape=jax.ShapeDtypeStruct((merged // 64, dirs, cols * 64), jnp.bfloat16),
        compiler_params=params(60 * 1024 * 1024),
        name="regroup",
    )(views)


def field_kernel(rays_ref, cos_ref, sin_ref, inner_ref, outer_ref, *out_refs):
    phase_cos = cos_ref[...]
    phase_sin = sin_ref[...]
    inner = inner_ref[...]
    outer = outer_ref[...]
    count = outer.shape[0] // 2
    each = count // 4
    groups = rays_ref.shape[1]
    stacked = []
    for group in range(groups):
        rays = rays_ref[:, group].reshape(DIRS, 32 * DIRS)

        def wave(tile):
            amplitude = rays[:, 128 * tile : 128 * (tile + 1)].astype(jnp.float32)
            wave_re = (amplitude * phase_cos).astype(jnp.bfloat16)
            wave_im = (amplitude * phase_sin).astype(jnp.bfloat16)
            return jnp.concatenate([wave_re, wave_im], axis=1)

        parts = []
        for low in range(8):
            waves = jnp.concatenate([wave(2 * low), wave(2 * low + 1)], axis=0)
            part = jnp.dot(waves, inner, preferred_element_type=jnp.float32)
            parts.append(part.astype(jnp.bfloat16))
        for part in parts:
            left = jnp.concatenate([part[:DIRS, :128], part[:DIRS, 128:]], axis=0)
            right = jnp.concatenate([part[DIRS:, :128], part[DIRS:, 128:]], axis=0)
            stacked.append(jnp.concatenate([left, right], axis=1))
    field = [jnp.dot(outer, s, preferred_element_type=jnp.float32) for s in stacked]
    for group in range(groups):
        own = field[8 * group : 8 * (group + 1)]
        sides = []
        for rows in (slice(0, count), slice(count, 2 * count)):
            sides.append(jnp.swapaxes(jnp.stack([f[rows] for f in own]), 0, 1))
        block = jnp.concatenate(sides, axis=1).astype(jnp.bfloat16)
        for partner in range(4):
            out_refs[partner][group] = block[each * partner : each * (partner + 1)]


def fields(rays, phase_cos, phase_sin, inner, outer, start, groups, step=2):
    count = outer.shape[0] // 2
    whole = lambda i: (0, 0)
    out_block = pl.BlockSpec((step, count // 4, 16, 256), lambda i: (i, 0, 0, 0))
    return pl.pallas_call(
        field_kernel,
        grid=(groups // step,),
        in_specs=[
            pl.BlockSpec((4, step, 16, 2048), lambda i: (0, start // step + i, 0, 0)),
            pl.BlockSpec((DIRS, 128), whole),
            pl.BlockSpec((DIRS, 128), whole),
            pl.BlockSpec((256, 256), whole),
            pl.BlockSpec((2 * count, 128), whole),
        ],
        out_specs=[out_block] * 4,
        out_shape=[jax.ShapeDtypeStruct((groups, count // 4, 16, 256), jnp.bfloat16)] * 4,
        compiler_params=params(),
        cost_estimate=pl.CostEstimate(
            flops=2 * 10**9, bytes_accessed=4 * 2**20, transcendentals=0
        ),
        name="fields",
    )(rays, phase_cos, phase_sin, inner, outer)


def spectrum_kernel(count, filled, *refs):
    pieces, tables = refs[:count], refs[count : count + 6]
    first_ref, twist_re_ref, twist_im_ref, second_ref, turn_re_ref, turn_im_ref = tables
    re_ref, im_ref, turned_ref = refs[count + 6 + filled :]
    rows = turned_ref.shape[0]

    @pl.when(pl.program_id(0) == 0)
    def _():
        for row in range(rows):
            signal = [p[:, row].reshape(-1, SIDE) for p in pieces]
            signal = jnp.concatenate(signal, axis=0)
            section = jnp.dot(first_ref[...], signal, preferred_element_type=jnp.float32)
            section_re, section_im = section[:SIDE], section[SIDE:]
            twist_re, twist_im = twist_re_ref[...], twist_im_ref[...]
            turned_re = section_re * twist_re - section_im * twist_im
            turned_im = section_re * twist_im + section_im * twist_re
            turned_ref[row, :, :SIDE] = turned_re.astype(jnp.bfloat16)
            turned_ref[row, :, SIDE:] = turned_im.astype(jnp.bfloat16)

    half = SIDE // 2
    second = second_ref[...].reshape(2 * half, 2 * SIDE)
    for row in range(rows):
        final = lax.dot_general(
            second,
            turned_ref[row],
            (((1,), (1,)), ((), ())),
            preferred_element_type=jnp.float32,
        )
        final_re, final_im = final[:half], final[half:]
        turn_re, turn_im = turn_re_ref[...], turn_im_ref[...]
        out_re = final_re * turn_re - final_im * turn_im
        out_im = final_re * turn_im + final_im * turn_re
        for side in range(2):
            lanes = slice(128 * side, 128 * (side + 1))
            place = pl.ds(8 * side + row, half, stride=16)
            re_ref[place, :] = out_re[:, lanes]
            im_ref[place, :] = out_im[:, lanes]


def spectra(pieces, tables, half, filled):
    count, rows = len(pieces), pieces[0].shape[1]
    whole = lambda i: (0, 0)
    piece_specs = [pl.BlockSpec(p.shape, lambda i: (0, 0, 0, 0)) for p in pieces]
    square = pl.BlockSpec((SIDE, SIDE), whole)
    first = pl.BlockSpec((2 * SIDE, 2 * SIDE), whole)
    second = pl.BlockSpec((2, SIDE // 2, 2 * SIDE), lambda i: (0, i, 0))
    turn = pl.BlockSpec((SIDE // 2, SIDE), lambda i: (i, 0))
    out_block = pl.BlockSpec((8 * SIDE, 128), lambda i: (2 * half + i, 0))
    out_shape = jax.ShapeDtypeStruct((2 * 16 * SIDE, 128), jnp.float32)
    aliases = {count + 6 + i: i for i in range(len(filled))}
    return pl.pallas_call(
        functools.partial(spectrum_kernel, count, len(filled)),
        grid=(2,),
        in_specs=piece_specs
        + [first, square, square, second, turn, turn]
        + [pl.BlockSpec(memory_space=pl.ANY)] * len(filled),
        out_specs=[out_block, out_block],
        out_shape=[out_shape, out_shape],
        scratch_shapes=[pltpu.VMEM((rows, SIDE, 2 * SIDE), jnp.bfloat16)],
        input_output_aliases=aliases,
        compiler_params=params(),
        cost_estimate=pl.CostEstimate(
            flops=8 * 10**9, bytes_accessed=8 * 2**20, transcendentals=0
        ),
        name="spectra",
    )(*pieces, *tables, *filled)


def inner_outer_tables():
    table_re, table_im = direction_table(DIRS)
    zero = jnp.zeros_like(table_re)
    twice = lambda t: jnp.block([[t, zero], [zero, t]])
    inner = jnp.block(
        [[twice(table_re), twice(table_im)], [twice(-table_im), twice(table_re)]]
    )
    outer = jnp.stack(
        [
            jnp.concatenate([table_re, -table_im], axis=1),
            jnp.concatenate([table_im, table_re], axis=1),
        ]
    )
    return inner, outer.reshape(2, 4, 2, 8, 2 * DIRS)


def first_tables():
    source = np.arange(4)[:, None, None]
    group = np.arange(8)[None, :, None]
    low = np.arange(8)[None, None, :]
    places = 32 * group + 8 * source + low
    cosine, sine = numpy_turns(np.arange(SIDE), places.reshape(-1), SIDE)
    shape = (SIDE, 4, 8, 8)
    cosine = cosine.reshape(shape) / 16.0
    sine = sine.reshape(shape) / 16.0
    upper = np.stack([cosine, sine], axis=3)
    lower = np.stack([-sine, cosine], axis=3)
    table = np.concatenate([upper, lower], axis=0).reshape(2 * SIDE, 4, 128)
    return jnp.asarray(table.transpose(1, 0, 2), dtype=jnp.bfloat16)


def second_table():
    cosine, sine = numpy_turns(np.arange(SIDE), np.arange(SIDE), SIDE)
    table = np.block([[cosine, sine], [-sine, cosine]]) / 16.0
    return jnp.asarray(table.reshape(2, SIDE, 2 * SIDE), dtype=jnp.bfloat16)


def twist_tables():
    cosine, sine = numpy_turns(np.arange(SIDE), np.arange(SIDE), SIDE * SIDE)
    return jnp.asarray(cosine, dtype=jnp.float32), jnp.asarray(-sine, dtype=jnp.float32)


def to_rows(flat):
    rows = flat.shape[0] // (16 * SIDE) * 8
    tiles = flat.reshape(rows // 8, SIDE, 2, 8, 128)
    return tiles.transpose(0, 3, 1, 2, 4).reshape(rows, SIDE * SIDE)


def per_device(views, phases, kernel_phase):
    sent = regroup(views)
    rays = lax.all_to_all(sent, HOGEL_GROUP, split_axis=0, concat_axis=0, tiled=True)
    rays = rays.reshape(4, 8, 16, 2048)
    angles = phases.astype(jnp.float32) * (2.0 * math.pi / PHASES)
    phase_cos = jnp.tile(jnp.cos(angles), (1, 2))
    phase_sin = jnp.tile(jnp.sin(angles), (1, 2))
    inner, outer = inner_outer_tables()
    me = lax.axis_index("zl") * 2 + lax.axis_index("xl")
    partners = [me ^ d for d in range(4)]
    pick = lambda table, at, axis: lax.dynamic_index_in_dim(table, at, axis, False)
    outer = jnp.stack([pick(outer, at, 1) for at in partners], axis=1)
    source_tables = first_tables()
    first = jnp.concatenate([pick(source_tables, at, 0) for at in partners], axis=1)
    twist_re, twist_im = twist_tables()
    turn = kernel_phase.reshape(SIDE, SIDE)
    tables = (first, twist_re, twist_im, second_table(), jnp.cos(turn), jnp.sin(turn))
    halves = []
    for half, starts in enumerate(((0, 4, 8), (0, 8))):
        outer_half = outer[:, :, half].reshape(2 * 4 * 8, 2 * DIRS)
        pieces = [[] for _ in range(4)]
        for start, end in zip(starts[:-1], starts[1:]):
            sending = fields(
                rays, phase_cos, phase_sin, inner, outer_half, start, end - start
            )
            pieces[0].append(sending[0])
            for d in (3, 1, 2):
                swaps = [(i, i ^ d) for i in range(4)]
                pieces[d].append(lax.ppermute(sending[d], SQUARE, swaps))
        halves.append([p for partner in pieces for p in partner])
    filled = spectra(halves[0], tables, 0, ())
    flat_re, flat_im = spectra(halves[1], tables, 1, filled)
    return to_rows(flat_re), to_rows(flat_im)


def solution(mesh):
    fine = Mesh(mesh.devices.reshape(2, 2, 4, 2, 2, 2), VIEW + COL)
    in_specs = (P(VIEW, COL, None), P(), P())
    out_specs = (P(VIEW + COL, None), P(VIEW + COL, None))
    return jax.shard_map(
        per_device, mesh=fine, in_specs=in_specs, out_specs=out_specs, check_vma=False
    )
```

```python
import functools
import math

import jax
import jax.numpy as jnp
import numpy as np
from jax import lax
from jax.experimental import pallas as pl
from jax.experimental.pallas import tpu as pltpu
from jax.sharding import Mesh
from jax.sharding import PartitionSpec as P

PHASES = 256
DIRS = 64
SIDE = 256
VIEW = ("xh", "co")
COL = ("y", "zh", "zl", "xl")
HOGEL_ORDER = (
    29, 5, 15, 12, 24, 14, 31, 11, 16, 30, 13, 8, 4, 1, 6, 23,
    0, 21, 26, 2, 22, 28, 19, 17, 3, 10, 7, 9, 18, 27, 25, 20,
)
RANK_OF = tuple(HOGEL_ORDER.index(row) for row in range(len(HOGEL_ORDER)))
SQUARE = ("zl", "xl")
VMEM_BYTES = 40 * 1024 * 1024


def direction_table(length):
    positions = jnp.arange(length, dtype=jnp.int32)
    angles = (positions[:, None] * positions[None, :] % length).astype(jnp.float32) * (
        2.0 * math.pi / length
    )
    factor = 1.0 / math.sqrt(length)
    return (
        (jnp.cos(angles) * factor).astype(jnp.bfloat16),
        (jnp.sin(angles) * factor).astype(jnp.bfloat16),
    )


def numpy_turns(first, second, modulus):
    angles = (np.outer(first, second) % modulus) * (2.0 * np.pi / modulus)
    return np.cos(angles), np.sin(angles)


def params(limit=VMEM_BYTES):
    return pltpu.CompilerParams(
        dimension_semantics=("arbitrary",), vmem_limit_bytes=limit
    )


def regroup_kernel(views_ref, out_ref):
    dirs, cols, lanes = views_ref.shape
    for pair in range(lanes // 128):
        block = jnp.swapaxes(views_ref[:, :, 128 * pair : 128 * (pair + 1)], 0, 1)
        for col in range(0, cols, 2):
            even, odd = block[col], block[col + 1]
            place = slice(64 * col, 64 * col + 128)
            for side in range(2):
                own = slice(64 * side, 64 * (side + 1))
                joined = jnp.concatenate([even[:, own], odd[:, own]], axis=1)
                out_ref[RANK_OF[2 * pair + side], :, place] = joined


def regroup(views, steps=2):
    dirs, cols, merged = views.shape
    each = cols // steps
    return pl.pallas_call(
        regroup_kernel,
        grid=(steps,),
        in_specs=[pl.BlockSpec((dirs, each, merged), lambda i: (0, i, 0))],
        out_specs=pl.BlockSpec((merged // 64, dirs, each * 64), lambda i: (0, 0, i)),
        out_shape=jax.ShapeDtypeStruct((merged // 64, dirs, cols * 64), jnp.bfloat16),
        compiler_params=params(60 * 1024 * 1024),
        name="regroup",
    )(views)


def field_kernel(place_ref, *refs):
    rays_refs, out_refs = refs[:-8], refs[-4:]
    cos_ref, sin_ref, inner_ref, outer_ref = refs[-8:-4]
    phase_cos = cos_ref[...]
    phase_sin = sin_ref[...]
    inner = inner_ref[...]
    outer = outer_ref[...]
    count = outer.shape[0] // 2
    each = count // 4
    groups = len(rays_refs) // 4
    stacked = []
    for group in range(groups):
        own = rays_refs[4 * group : 4 * (group + 1)]
        rays = jnp.concatenate([r[0] for r in own], axis=0)

        def wave(tile):
            amplitude = rays[:, 128 * tile : 128 * (tile + 1)].astype(jnp.float32)
            wave_re = (amplitude * phase_cos).astype(jnp.bfloat16)
            wave_im = (amplitude * phase_sin).astype(jnp.bfloat16)
            return jnp.concatenate([wave_re, wave_im], axis=1)

        parts = []
        for low in range(8):
            waves = jnp.concatenate([wave(2 * low), wave(2 * low + 1)], axis=0)
            part = jnp.dot(waves, inner, preferred_element_type=jnp.float32)
            parts.append(part.astype(jnp.bfloat16))
        for part in parts:
            left = jnp.concatenate([part[:DIRS, :128], part[:DIRS, 128:]], axis=0)
            right = jnp.concatenate([part[DIRS:, :128], part[DIRS:, 128:]], axis=0)
            stacked.append(jnp.concatenate([left, right], axis=1))
    field = [jnp.dot(outer, s, preferred_element_type=jnp.float32) for s in stacked]
    for group in range(groups):
        own = field[8 * group : 8 * (group + 1)]
        sides = []
        for rows in (slice(0, count), slice(count, 2 * count)):
            sides.append(jnp.swapaxes(jnp.stack([f[rows] for f in own]), 0, 1))
        block = jnp.concatenate(sides, axis=1).astype(jnp.bfloat16)
        for partner in range(4):
            out_refs[partner][group] = block[each * partner : each * (partner + 1)]


def fields(rays, phase_cos, phase_sin, inner, outer, start, groups, step=2):
    count = outer.shape[0] // 2
    whole = lambda i, place: (0, 0)
    out_block = pl.BlockSpec(
        (step, count // 4, 16, 256), lambda i, place: (i, 0, 0, 0)
    )
    out_shape = jax.ShapeDtypeStruct((groups, count // 4, 16, 256), jnp.bfloat16)

    def source(group, view):
        at = lambda i, place: (place[8 * view + start + step * i + group], 0, 0)
        return pl.BlockSpec((1, 16, 2048), at)

    sources = [source(group, view) for group in range(step) for view in range(4)]
    return pl.pallas_call(
        field_kernel,
        grid_spec=pltpu.PrefetchScalarGridSpec(
            num_scalar_prefetch=1,
            grid=(groups // step,),
            in_specs=sources
            + [
                pl.BlockSpec((DIRS, 128), whole),
                pl.BlockSpec((DIRS, 128), whole),
                pl.BlockSpec((256, 256), whole),
                pl.BlockSpec((2 * count, 128), whole),
            ],
            out_specs=[out_block] * 4,
        ),
        out_shape=[out_shape] * 4,
        compiler_params=params(),
        cost_estimate=pl.CostEstimate(
            flops=2 * 10**9, bytes_accessed=4 * 2**20, transcendentals=0
        ),
        name="fields",
    )(
        jnp.asarray(RANK_OF, jnp.int32),
        *[rays] * len(sources),
        phase_cos,
        phase_sin,
        inner,
        outer,
    )


def spectrum_kernel(count, filled, *refs):
    pieces, tables = refs[:count], refs[count : count + 6]
    first_ref, twist_re_ref, twist_im_ref, second_ref, turn_re_ref, turn_im_ref = tables
    re_ref, im_ref, turned_ref = refs[count + 6 + filled :]
    rows = turned_ref.shape[0]

    @pl.when(pl.program_id(0) == 0)
    def _():
        for row in range(rows):
            signal = [p[:, row].reshape(-1, SIDE) for p in pieces]
            signal = jnp.concatenate(signal, axis=0)
            section = jnp.dot(first_ref[...], signal, preferred_element_type=jnp.float32)
            section_re, section_im = section[:SIDE], section[SIDE:]
            twist_re, twist_im = twist_re_ref[...], twist_im_ref[...]
            turned_re = section_re * twist_re - section_im * twist_im
            turned_im = section_re * twist_im + section_im * twist_re
            turned_ref[row, :, :SIDE] = turned_re.astype(jnp.bfloat16)
            turned_ref[row, :, SIDE:] = turned_im.astype(jnp.bfloat16)

    half = SIDE // 2
    second = second_ref[...].reshape(2 * half, 2 * SIDE)
    for row in range(rows):
        final = lax.dot_general(
            second,
            turned_ref[row],
            (((1,), (1,)), ((), ())),
            preferred_element_type=jnp.float32,
        )
        final_re, final_im = final[:half], final[half:]
        turn_re, turn_im = turn_re_ref[...], turn_im_ref[...]
        out_re = final_re * turn_re - final_im * turn_im
        out_im = final_re * turn_im + final_im * turn_re
        for side in range(2):
            lanes = slice(128 * side, 128 * (side + 1))
            place = pl.ds(8 * side + row, half, stride=16)
            re_ref[place, :] = out_re[:, lanes]
            im_ref[place, :] = out_im[:, lanes]


def spectra(pieces, tables, half, filled):
    count, rows = len(pieces), pieces[0].shape[1]
    whole = lambda i: (0, 0)
    piece_specs = [pl.BlockSpec(p.shape, lambda i: (0, 0, 0, 0)) for p in pieces]
    square = pl.BlockSpec((SIDE, SIDE), whole)
    first = pl.BlockSpec((2 * SIDE, 2 * SIDE), whole)
    second = pl.BlockSpec((2, SIDE // 2, 2 * SIDE), lambda i: (0, i, 0))
    turn = pl.BlockSpec((SIDE // 2, SIDE), lambda i: (i, 0))
    out_block = pl.BlockSpec((8 * SIDE, 128), lambda i: (2 * half + i, 0))
    out_shape = jax.ShapeDtypeStruct((2 * 16 * SIDE, 128), jnp.float32)
    aliases = {count + 6 + i: i for i in range(len(filled))}
    return pl.pallas_call(
        functools.partial(spectrum_kernel, count, len(filled)),
        grid=(2,),
        in_specs=piece_specs
        + [first, square, square, second, turn, turn]
        + [pl.BlockSpec(memory_space=pl.ANY)] * len(filled),
        out_specs=[out_block, out_block],
        out_shape=[out_shape, out_shape],
        scratch_shapes=[pltpu.VMEM((rows, SIDE, 2 * SIDE), jnp.bfloat16)],
        input_output_aliases=aliases,
        compiler_params=params(),
        cost_estimate=pl.CostEstimate(
            flops=8 * 10**9, bytes_accessed=8 * 2**20, transcendentals=0
        ),
        name="spectra",
    )(*pieces, *tables, *filled)


def inner_outer_tables():
    table_re, table_im = direction_table(DIRS)
    zero = jnp.zeros_like(table_re)
    twice = lambda t: jnp.block([[t, zero], [zero, t]])
    inner = jnp.block(
        [[twice(table_re), twice(table_im)], [twice(-table_im), twice(table_re)]]
    )
    outer = jnp.stack(
        [
            jnp.concatenate([table_re, -table_im], axis=1),
            jnp.concatenate([table_im, table_re], axis=1),
        ]
    )
    return inner, outer.reshape(2, 4, 2, 8, 2 * DIRS)


def first_tables():
    source = np.arange(4)[:, None, None]
    group = np.arange(8)[None, :, None]
    low = np.arange(8)[None, None, :]
    places = 32 * group + 8 * source + low
    cosine, sine = numpy_turns(np.arange(SIDE), places.reshape(-1), SIDE)
    shape = (SIDE, 4, 8, 8)
    cosine = cosine.reshape(shape) / 16.0
    sine = sine.reshape(shape) / 16.0
    upper = np.stack([cosine, sine], axis=3)
    lower = np.stack([-sine, cosine], axis=3)
    table = np.concatenate([upper, lower], axis=0).reshape(2 * SIDE, 4, 128)
    return jnp.asarray(table.transpose(1, 0, 2), dtype=jnp.bfloat16)


def second_table():
    cosine, sine = numpy_turns(np.arange(SIDE), np.arange(SIDE), SIDE)
    table = np.block([[cosine, sine], [-sine, cosine]]) / 16.0
    return jnp.asarray(table.reshape(2, SIDE, 2 * SIDE), dtype=jnp.bfloat16)


def twist_tables():
    cosine, sine = numpy_turns(np.arange(SIDE), np.arange(SIDE), SIDE * SIDE)
    return jnp.asarray(cosine, dtype=jnp.float32), jnp.asarray(-sine, dtype=jnp.float32)


def to_rows(flat):
    rows = flat.shape[0] // (16 * SIDE) * 8
    tiles = flat.reshape(rows // 8, SIDE, 2, 8, 128)
    return tiles.transpose(0, 3, 1, 2, 4).reshape(rows, SIDE * SIDE)


def hogel_groups():
    return [[4 * row + at for row in HOGEL_ORDER] for at in range(4)]


def per_device(views, phases, kernel_phase):
    sent = regroup(views)
    rays = lax.all_to_all(
        sent, VIEW + COL, 0, 0, axis_index_groups=hogel_groups(), tiled=True
    )
    angles = phases.astype(jnp.float32) * (2.0 * math.pi / PHASES)
    phase_cos = jnp.tile(jnp.cos(angles), (1, 2))
    phase_sin = jnp.tile(jnp.sin(angles), (1, 2))
    inner, outer = inner_outer_tables()
    me = lax.axis_index("zl") * 2 + lax.axis_index("xl")
    partners = [me ^ d for d in range(4)]
    pick = lambda table, at, axis: lax.dynamic_index_in_dim(table, at, axis, False)
    outer = jnp.stack([pick(outer, at, 1) for at in partners], axis=1)
    source_tables = first_tables()
    first = jnp.concatenate([pick(source_tables, at, 0) for at in partners], axis=1)
    twist_re, twist_im = twist_tables()
    turn = kernel_phase.reshape(SIDE, SIDE)
    tables = (first, twist_re, twist_im, second_table(), jnp.cos(turn), jnp.sin(turn))
    halves = []
    for half, starts in enumerate(((0, 4, 8), (0, 8))):
        outer_half = outer[:, :, half].reshape(2 * 4 * 8, 2 * DIRS)
        pieces = [[] for _ in range(4)]
        for start, end in zip(starts[:-1], starts[1:]):
            sending = fields(
                rays, phase_cos, phase_sin, inner, outer_half, start, end - start
            )
            pieces[0].append(sending[0])
            for d in (3, 1, 2):
                swaps = [(i, i ^ d) for i in range(4)]
                pieces[d].append(lax.ppermute(sending[d], SQUARE, swaps))
        halves.append([p for partner in pieces for p in partner])
    filled = spectra(halves[0], tables, 0, ())
    flat_re, flat_im = spectra(halves[1], tables, 1, filled)
    return to_rows(flat_re), to_rows(flat_im)


def solution(mesh):
    fine = Mesh(mesh.devices.reshape(2, 2, 4, 2, 2, 2), VIEW + COL)
    in_specs = (P(VIEW, COL, None), P(), P())
    out_specs = (P(VIEW + COL, None), P(VIEW + COL, None))
    return jax.shard_map(
        per_device, mesh=fine, in_specs=in_specs, out_specs=out_specs, check_vma=False
    )
```

```python
import functools
import math

import jax
import jax.numpy as jnp
import numpy as np
from jax import lax
from jax.experimental import pallas as pl
from jax.experimental.pallas import tpu as pltpu
from jax.sharding import Mesh
from jax.sharding import PartitionSpec as P

PHASES = 256
DIRS = 64
SIDE = 256
VIEW = ("xh", "co")
COL = ("y", "zh", "zl", "xl")
HOGEL_ORDER = (
    29, 5, 15, 12, 24, 14, 31, 11, 16, 30, 13, 8, 4, 1, 6, 23,
    0, 21, 26, 2, 22, 28, 19, 17, 3, 10, 7, 9, 18, 27, 25, 20,
)
RANK_OF = tuple(HOGEL_ORDER.index(row) for row in range(len(HOGEL_ORDER)))
SQUARE = ("zl", "xl")
VMEM_BYTES = 40 * 1024 * 1024


def direction_table(length):
    positions = jnp.arange(length, dtype=jnp.int32)
    angles = (positions[:, None] * positions[None, :] % length).astype(jnp.float32) * (
        2.0 * math.pi / length
    )
    factor = 1.0 / math.sqrt(length)
    return (
        (jnp.cos(angles) * factor).astype(jnp.bfloat16),
        (jnp.sin(angles) * factor).astype(jnp.bfloat16),
    )


def numpy_turns(first, second, modulus):
    angles = (np.outer(first, second) % modulus) * (2.0 * np.pi / modulus)
    return np.cos(angles), np.sin(angles)


def params(limit=VMEM_BYTES):
    return pltpu.CompilerParams(
        dimension_semantics=("arbitrary",), vmem_limit_bytes=limit
    )


def regroup_kernel(views_ref, out_ref):
    dirs, cols, lanes = views_ref.shape
    for pair in range(lanes // 128):
        block = jnp.swapaxes(views_ref[:, :, 128 * pair : 128 * (pair + 1)], 0, 1)
        for col in range(0, cols, 2):
            even, odd = block[col], block[col + 1]
            place = slice(64 * col, 64 * col + 128)
            for side in range(2):
                own = slice(64 * side, 64 * (side + 1))
                joined = jnp.concatenate([even[:, own], odd[:, own]], axis=1)
                out_ref[RANK_OF[2 * pair + side], :, place] = joined


def regroup(views, steps=2):
    dirs, cols, merged = views.shape
    each = cols // steps
    return pl.pallas_call(
        regroup_kernel,
        grid=(steps,),
        in_specs=[pl.BlockSpec((dirs, each, merged), lambda i: (0, i, 0))],
        out_specs=pl.BlockSpec((merged // 64, dirs, each * 64), lambda i: (0, 0, i)),
        out_shape=jax.ShapeDtypeStruct((merged // 64, dirs, cols * 64), jnp.bfloat16),
        compiler_params=params(60 * 1024 * 1024),
        name="regroup",
    )(views)


def field_kernel(
    start, groups, place_ref, rays_ref, cos_ref, sin_ref, inner_ref, outer_ref, *out_refs
):
    begin = start + groups * pl.program_id(0)
    phase_cos = cos_ref[...]
    phase_sin = sin_ref[...]
    inner = inner_ref[...]
    outer = outer_ref[...]
    count = outer.shape[0] // 2
    each = count // 4
    stacked = []
    for group in range(groups):
        own = [rays_ref[place_ref[8 * view + begin + group]] for view in range(4)]
        rays = jnp.concatenate(own, axis=0)

        def wave(tile):
            amplitude = rays[:, 128 * tile : 128 * (tile + 1)].astype(jnp.float32)
            wave_re = (amplitude * phase_cos).astype(jnp.bfloat16)
            wave_im = (amplitude * phase_sin).astype(jnp.bfloat16)
            return jnp.concatenate([wave_re, wave_im], axis=1)

        parts = []
        for low in range(8):
            waves = jnp.concatenate([wave(2 * low), wave(2 * low + 1)], axis=0)
            part = jnp.dot(waves, inner, preferred_element_type=jnp.float32)
            parts.append(part.astype(jnp.bfloat16))
        for part in parts:
            left = jnp.concatenate([part[:DIRS, :128], part[:DIRS, 128:]], axis=0)
            right = jnp.concatenate([part[DIRS:, :128], part[DIRS:, 128:]], axis=0)
            stacked.append(jnp.concatenate([left, right], axis=1))
    field = [jnp.dot(outer, s, preferred_element_type=jnp.float32) for s in stacked]
    for group in range(groups):
        own = field[8 * group : 8 * (group + 1)]
        sides = []
        for rows in (slice(0, count), slice(count, 2 * count)):
            sides.append(jnp.swapaxes(jnp.stack([f[rows] for f in own]), 0, 1))
        block = jnp.concatenate(sides, axis=1).astype(jnp.bfloat16)
        for partner in range(4):
            out_refs[partner][group] = block[each * partner : each * (partner + 1)]


def fields(rays, phase_cos, phase_sin, inner, outer, start, groups, step=2):
    each = outer.shape[0] // 8
    in_vmem = pl.BlockSpec(memory_space=pltpu.VMEM)
    out_block = pl.BlockSpec((step, each, 16, 256), lambda i: (i, 0, 0, 0))
    out_shape = jax.ShapeDtypeStruct((groups, each, 16, 256), jnp.bfloat16)
    return pl.pallas_call(
        functools.partial(field_kernel, start, step),
        grid=(groups // step,),
        in_specs=[pl.BlockSpec(memory_space=pltpu.SMEM)] + [in_vmem] * 5,
        out_specs=[out_block] * 4,
        out_shape=[out_shape] * 4,
        compiler_params=params(),
        cost_estimate=pl.CostEstimate(
            flops=2 * 10**9, bytes_accessed=4 * 2**20, transcendentals=0
        ),
        name="fields",
    )(jnp.asarray(RANK_OF, jnp.int32), rays, phase_cos, phase_sin, inner, outer)


def spectrum_kernel(count, early, filled, keep, *refs):
    pieces, tables = refs[:count], refs[count : count + 6]
    first_ref, twist_re_ref, twist_im_ref, second_ref, turn_re_ref, turn_im_ref = tables
    early_refs = refs[count + 6 : count + 6 + early]
    re_ref, im_ref, turned_ref = refs[count + 6 + early + filled :]
    rows = turned_ref.shape[0]
    half = SIDE // 2

    @pl.when(pl.program_id(0) == 0)
    def _():
        for row in range(rows):
            signal = [p[:, row].reshape(-1, SIDE) for p in pieces]
            signal = jnp.concatenate(signal, axis=0)
            section = jnp.dot(first_ref[...], signal, preferred_element_type=jnp.float32)
            section_re, section_im = section[:SIDE], section[SIDE:]
            twist_re, twist_im = twist_re_ref[...], twist_im_ref[...]
            turned_re = section_re * twist_re - section_im * twist_im
            turned_im = section_re * twist_im + section_im * twist_re
            turned_ref[row, :, :SIDE] = turned_re.astype(jnp.bfloat16)
            turned_ref[row, :, SIDE:] = turned_im.astype(jnp.bfloat16)

    def place_row(row, out_re, out_im):
        for side in range(2):
            lanes = slice(128 * side, 128 * (side + 1))
            place = pl.ds(8 * side + row, half, stride=16)
            re_ref[place, :] = out_re[:, lanes]
            im_ref[place, :] = out_im[:, lanes]

    second = second_ref[...].reshape(2 * half, 2 * SIDE)
    for row in range(rows):
        final = lax.dot_general(
            second,
            turned_ref[row],
            (((1,), (1,)), ((), ())),
            preferred_element_type=jnp.float32,
        )
        final_re, final_im = final[:half], final[half:]
        turn_re, turn_im = turn_re_ref[...], turn_im_ref[...]
        out_re = final_re * turn_re - final_im * turn_im
        out_im = final_re * turn_im + final_im * turn_re
        if keep:
            re_ref[row] = out_re
            im_ref[row] = out_im
        else:
            place_row(8 - rows + row, out_re, out_im)
    if early:
        for row in range(8 - rows):
            place_row(row, early_refs[0][row], early_refs[1][row])


def spectra(pieces, tables, half, early=(), filled=()):
    count, rows = len(pieces), pieces[0].shape[1]
    keep = half is None
    whole = lambda i: (0, 0)
    piece_specs = [pl.BlockSpec(p.shape, lambda i: (0, 0, 0, 0)) for p in pieces]
    square = pl.BlockSpec((SIDE, SIDE), whole)
    first = pl.BlockSpec((2 * SIDE, 2 * SIDE), whole)
    second = pl.BlockSpec((2, SIDE // 2, 2 * SIDE), lambda i: (0, i, 0))
    turn = pl.BlockSpec((SIDE // 2, SIDE), lambda i: (i, 0))
    kept_spec = lambda n: pl.BlockSpec((n, SIDE // 2, SIDE), lambda i: (0, i, 0))
    if keep:
        out_block = kept_spec(rows)
        out_shape = jax.ShapeDtypeStruct((rows, SIDE, SIDE), jnp.float32)
    else:
        out_block = pl.BlockSpec((8 * SIDE, 128), lambda i: (2 * half + i, 0))
        out_shape = jax.ShapeDtypeStruct((2 * 16 * SIDE, 128), jnp.float32)
    aliases = {count + 6 + len(early) + i: i for i in range(len(filled))}
    return pl.pallas_call(
        functools.partial(spectrum_kernel, count, len(early), len(filled), keep),
        grid=(2,),
        in_specs=piece_specs
        + [first, square, square, second, turn, turn]
        + [kept_spec(8 - rows)] * len(early)
        + [pl.BlockSpec(memory_space=pl.ANY)] * len(filled),
        out_specs=[out_block, out_block],
        out_shape=[out_shape, out_shape],
        scratch_shapes=[pltpu.VMEM((rows, SIDE, 2 * SIDE), jnp.bfloat16)],
        input_output_aliases=aliases,
        compiler_params=params(),
        cost_estimate=pl.CostEstimate(
            flops=10**9 * rows, bytes_accessed=2**20 * rows, transcendentals=0
        ),
        name="spectra",
    )(*pieces, *tables, *early, *filled)


def inner_outer_tables():
    table_re, table_im = direction_table(DIRS)
    zero = jnp.zeros_like(table_re)
    twice = lambda t: jnp.block([[t, zero], [zero, t]])
    inner = jnp.block(
        [[twice(table_re), twice(table_im)], [twice(-table_im), twice(table_re)]]
    )
    outer = jnp.stack(
        [
            jnp.concatenate([table_re, -table_im], axis=1),
            jnp.concatenate([table_im, table_re], axis=1),
        ]
    )
    return inner, outer.reshape(2, 4, 16, 2 * DIRS)


def first_tables():
    source = np.arange(4)[:, None, None]
    group = np.arange(8)[None, :, None]
    low = np.arange(8)[None, None, :]
    places = 32 * group + 8 * source + low
    cosine, sine = numpy_turns(np.arange(SIDE), places.reshape(-1), SIDE)
    shape = (SIDE, 4, 8, 8)
    cosine = cosine.reshape(shape) / 16.0
    sine = sine.reshape(shape) / 16.0
    upper = np.stack([cosine, sine], axis=3)
    lower = np.stack([-sine, cosine], axis=3)
    table = np.concatenate([upper, lower], axis=0).reshape(2 * SIDE, 4, 128)
    return jnp.asarray(table.transpose(1, 0, 2), dtype=jnp.bfloat16)


def second_table():
    cosine, sine = numpy_turns(np.arange(SIDE), np.arange(SIDE), SIDE)
    table = np.block([[cosine, sine], [-sine, cosine]]) / 16.0
    return jnp.asarray(table.reshape(2, SIDE, 2 * SIDE), dtype=jnp.bfloat16)


def twist_tables():
    cosine, sine = numpy_turns(np.arange(SIDE), np.arange(SIDE), SIDE * SIDE)
    return jnp.asarray(cosine, dtype=jnp.float32), jnp.asarray(-sine, dtype=jnp.float32)


def to_rows(flat):
    rows = flat.shape[0] // (16 * SIDE) * 8
    tiles = flat.reshape(rows // 8, SIDE, 2, 8, 128)
    return tiles.transpose(0, 3, 1, 2, 4).reshape(rows, SIDE * SIDE)


def hogel_groups():
    return [[4 * row + at for row in HOGEL_ORDER] for at in range(4)]


def per_device(views, phases, kernel_phase):
    sent = regroup(views)
    rays = lax.all_to_all(
        sent, VIEW + COL, 0, 0, axis_index_groups=hogel_groups(), tiled=True
    )
    angles = phases.astype(jnp.float32) * (2.0 * math.pi / PHASES)
    phase_cos = jnp.tile(jnp.cos(angles), (1, 2))
    phase_sin = jnp.tile(jnp.sin(angles), (1, 2))
    inner, outer = inner_outer_tables()
    me = lax.axis_index("zl") * 2 + lax.axis_index("xl")
    partners = [me ^ d for d in range(4)]
    pick = lambda table, at, axis: lax.dynamic_index_in_dim(table, at, axis, False)
    outer = jnp.stack([pick(outer, at, 1) for at in partners], axis=1)
    source_tables = first_tables()
    first = jnp.concatenate([pick(source_tables, at, 0) for at in partners], axis=1)
    twist_re, twist_im = twist_tables()
    turn = kernel_phase.reshape(SIDE, SIDE)
    tables = (first, twist_re, twist_im, second_table(), jnp.cos(turn), jnp.sin(turn))
    parts = []
    for rows, starts in (((0, 8), (0, 4, 8)), ((8, 12), (0, 8)), ((12, 16), (0, 8))):
        outer_part = outer[:, :, rows[0] : rows[1]].reshape(-1, 2 * DIRS)
        pieces = [[] for _ in range(4)]
        for start, end in zip(starts[:-1], starts[1:]):
            sending = fields(
                rays, phase_cos, phase_sin, inner, outer_part, start, end - start
            )
            pieces[0].append(sending[0])
            for d in (3, 1, 2):
                swaps = [(i, i ^ d) for i in range(4)]
                pieces[d].append(lax.ppermute(sending[d], SQUARE, swaps))
        parts.append([p for partner in pieces for p in partner])
    filled = spectra(parts[0], tables, 0)
    early = spectra(parts[1], tables, None)
    flat_re, flat_im = spectra(parts[2], tables, 1, early, filled)
    return to_rows(flat_re), to_rows(flat_im)


def solution(mesh):
    fine = Mesh(mesh.devices.reshape(2, 2, 4, 2, 2, 2), VIEW + COL)
    in_specs = (P(VIEW, COL, None), P(), P())
    out_specs = (P(VIEW + COL, None), P(VIEW + COL, None))
    return jax.shard_map(
        per_device, mesh=fine, in_specs=in_specs, out_specs=out_specs, check_vma=False
    )
```

```python
import functools
import math

import jax
import jax.numpy as jnp
import numpy as np
from jax import lax
from jax.experimental import pallas as pl
from jax.experimental.pallas import tpu as pltpu
from jax.sharding import Mesh
from jax.sharding import PartitionSpec as P

PHASES = 256
DIRS = 64
SIDE = 256
VIEW = ("xh", "co")
COL = ("y", "zh", "zl", "xl")
HOGEL_ORDER = (
    29, 5, 15, 12, 24, 14, 31, 11, 16, 30, 13, 8, 4, 1, 6, 23,
    0, 21, 26, 2, 22, 28, 19, 17, 3, 10, 7, 9, 18, 27, 25, 20,
)
RANK_OF = tuple(HOGEL_ORDER.index(row) for row in range(len(HOGEL_ORDER)))
SQUARE = ("zl", "xl")
VMEM_BYTES = 40 * 1024 * 1024


def direction_table(length):
    positions = jnp.arange(length, dtype=jnp.int32)
    angles = (positions[:, None] * positions[None, :] % length).astype(jnp.float32) * (
        2.0 * math.pi / length
    )
    factor = 1.0 / math.sqrt(length)
    return (
        (jnp.cos(angles) * factor).astype(jnp.bfloat16),
        (jnp.sin(angles) * factor).astype(jnp.bfloat16),
    )


def numpy_turns(first, second, modulus):
    angles = (np.outer(first, second) % modulus) * (2.0 * np.pi / modulus)
    return np.cos(angles), np.sin(angles)


def params(limit=VMEM_BYTES):
    return pltpu.CompilerParams(
        dimension_semantics=("arbitrary",), vmem_limit_bytes=limit
    )


def regroup_kernel(views_ref, out_ref):
    dirs, cols, lanes = views_ref.shape
    for pair in range(lanes // 128):
        block = jnp.swapaxes(views_ref[:, :, 128 * pair : 128 * (pair + 1)], 0, 1)
        for col in range(0, cols, 2):
            even, odd = block[col], block[col + 1]
            place = slice(64 * col, 64 * col + 128)
            for side in range(2):
                own = slice(64 * side, 64 * (side + 1))
                joined = jnp.concatenate([even[:, own], odd[:, own]], axis=1)
                out_ref[RANK_OF[2 * pair + side], :, place] = joined


def regroup(views, steps=2):
    dirs, cols, merged = views.shape
    each = cols // steps
    return pl.pallas_call(
        regroup_kernel,
        grid=(steps,),
        in_specs=[pl.BlockSpec((dirs, each, merged), lambda i: (0, i, 0))],
        out_specs=pl.BlockSpec((merged // 64, dirs, each * 64), lambda i: (0, 0, i)),
        out_shape=jax.ShapeDtypeStruct((merged // 64, dirs, cols * 64), jnp.bfloat16),
        compiler_params=params(60 * 1024 * 1024),
        name="regroup",
    )(views)


def field_kernel(
    start, groups, step, rays_ref, cos_ref, sin_ref, inner_ref, outer_ref, *out_refs
):
    phase_cos = cos_ref[...]
    phase_sin = sin_ref[...]
    inner = inner_ref[...]
    outer = outer_ref[...]
    count = outer.shape[0] // 2
    each = count // 4

    def partials(group):
        own = [rays_ref[RANK_OF[8 * view + start + group]] for view in range(4)]
        rays = jnp.concatenate(own, axis=0)

        def wave(tile):
            amplitude = rays[:, 128 * tile : 128 * (tile + 1)].astype(jnp.float32)
            wave_re = (amplitude * phase_cos).astype(jnp.bfloat16)
            wave_im = (amplitude * phase_sin).astype(jnp.bfloat16)
            return jnp.concatenate([wave_re, wave_im], axis=1)

        parts = []
        for low in range(8):
            waves = jnp.concatenate([wave(2 * low), wave(2 * low + 1)], axis=0)
            part = jnp.dot(waves, inner, preferred_element_type=jnp.float32)
            parts.append(part.astype(jnp.bfloat16))
        return parts

    for begin in range(0, groups, step):
        stacked = []
        for group in range(begin, begin + step):
            for part in partials(group):
                left = jnp.concatenate([part[:DIRS, :128], part[:DIRS, 128:]], axis=0)
                right = jnp.concatenate([part[DIRS:, :128], part[DIRS:, 128:]], axis=0)
                stacked.append(jnp.concatenate([left, right], axis=1))
        field = [jnp.dot(outer, s, preferred_element_type=jnp.float32) for s in stacked]
        for at in range(step):
            own = field[8 * at : 8 * (at + 1)]
            sides = []
            for rows in (slice(0, count), slice(count, 2 * count)):
                sides.append(jnp.swapaxes(jnp.stack([f[rows] for f in own]), 0, 1))
            block = jnp.concatenate(sides, axis=1).astype(jnp.bfloat16)
            for partner in range(4):
                out_refs[partner][begin + at] = block[each * partner : each * (partner + 1)]


def fields(rays, phase_cos, phase_sin, inner, outer, start, groups, step=4):
    each = outer.shape[0] // 8
    in_vmem = pl.BlockSpec(memory_space=pltpu.VMEM)
    out_shape = jax.ShapeDtypeStruct((groups, each, 16, 256), jnp.bfloat16)
    return pl.pallas_call(
        functools.partial(field_kernel, start, groups, step),
        in_specs=[in_vmem] * 5,
        out_specs=[in_vmem] * 4,
        out_shape=[out_shape] * 4,
        compiler_params=pltpu.CompilerParams(vmem_limit_bytes=VMEM_BYTES),
        cost_estimate=pl.CostEstimate(
            flops=2 * 10**9, bytes_accessed=4 * 2**20, transcendentals=0
        ),
        name="fields",
    )(rays, phase_cos, phase_sin, inner, outer)


def spectrum_kernel(count, early, filled, keep, *refs):
    pieces, tables = refs[:count], refs[count : count + 6]
    first_ref, twist_re_ref, twist_im_ref, second_ref, turn_re_ref, turn_im_ref = tables
    early_refs = refs[count + 6 : count + 6 + early]
    re_ref, im_ref, turned_ref = refs[count + 6 + early + filled :]
    rows = turned_ref.shape[0]
    half = SIDE // 2

    @pl.when(pl.program_id(0) == 0)
    def _():
        for row in range(rows):
            signal = [p[:, row].reshape(-1, SIDE) for p in pieces]
            signal = jnp.concatenate(signal, axis=0)
            section = jnp.dot(first_ref[...], signal, preferred_element_type=jnp.float32)
            section_re, section_im = section[:SIDE], section[SIDE:]
            twist_re, twist_im = twist_re_ref[...], twist_im_ref[...]
            turned_re = section_re * twist_re - section_im * twist_im
            turned_im = section_re * twist_im + section_im * twist_re
            turned_ref[row, :, :SIDE] = turned_re.astype(jnp.bfloat16)
            turned_ref[row, :, SIDE:] = turned_im.astype(jnp.bfloat16)

    def place_row(row, out_re, out_im):
        for side in range(2):
            lanes = slice(128 * side, 128 * (side + 1))
            place = pl.ds(8 * side + row, half, stride=16)
            re_ref[place, :] = out_re[:, lanes]
            im_ref[place, :] = out_im[:, lanes]

    second = second_ref[...].reshape(2 * half, 2 * SIDE)
    for row in range(rows):
        final = lax.dot_general(
            second,
            turned_ref[row],
            (((1,), (1,)), ((), ())),
            preferred_element_type=jnp.float32,
        )
        final_re, final_im = final[:half], final[half:]
        turn_re, turn_im = turn_re_ref[...], turn_im_ref[...]
        out_re = final_re * turn_re - final_im * turn_im
        out_im = final_re * turn_im + final_im * turn_re
        if keep:
            re_ref[row] = out_re
            im_ref[row] = out_im
        else:
            place_row(8 - rows + row, out_re, out_im)
    if early:
        for row in range(8 - rows):
            place_row(row, early_refs[0][row], early_refs[1][row])


def spectra(pieces, tables, half, early=(), filled=()):
    count, rows = len(pieces), pieces[0].shape[1]
    keep = half is None
    whole = lambda i: (0, 0)
    piece_specs = [pl.BlockSpec(p.shape, lambda i: (0, 0, 0, 0)) for p in pieces]
    square = pl.BlockSpec((SIDE, SIDE), whole)
    first = pl.BlockSpec((2 * SIDE, 2 * SIDE), whole)
    second = pl.BlockSpec((2, SIDE // 2, 2 * SIDE), lambda i: (0, i, 0))
    turn = pl.BlockSpec((SIDE // 2, SIDE), lambda i: (i, 0))
    kept_spec = lambda n: pl.BlockSpec((n, SIDE // 2, SIDE), lambda i: (0, i, 0))
    if keep:
        out_block = kept_spec(rows)
        out_shape = jax.ShapeDtypeStruct((rows, SIDE, SIDE), jnp.float32)
    else:
        out_block = pl.BlockSpec((8 * SIDE, 128), lambda i: (2 * half + i, 0))
        out_shape = jax.ShapeDtypeStruct((2 * 16 * SIDE, 128), jnp.float32)
    aliases = {count + 6 + len(early) + i: i for i in range(len(filled))}
    return pl.pallas_call(
        functools.partial(spectrum_kernel, count, len(early), len(filled), keep),
        grid=(2,),
        in_specs=piece_specs
        + [first, square, square, second, turn, turn]
        + [kept_spec(8 - rows)] * len(early)
        + [pl.BlockSpec(memory_space=pl.ANY)] * len(filled),
        out_specs=[out_block, out_block],
        out_shape=[out_shape, out_shape],
        scratch_shapes=[pltpu.VMEM((rows, SIDE, 2 * SIDE), jnp.bfloat16)],
        input_output_aliases=aliases,
        compiler_params=params(),
        cost_estimate=pl.CostEstimate(
            flops=10**9 * rows, bytes_accessed=2**20 * rows, transcendentals=0
        ),
        name="spectra",
    )(*pieces, *tables, *early, *filled)


def inner_outer_tables():
    table_re, table_im = direction_table(DIRS)
    zero = jnp.zeros_like(table_re)
    twice = lambda t: jnp.block([[t, zero], [zero, t]])
    inner = jnp.block(
        [[twice(table_re), twice(table_im)], [twice(-table_im), twice(table_re)]]
    )
    outer = jnp.stack(
        [
            jnp.concatenate([table_re, -table_im], axis=1),
            jnp.concatenate([table_im, table_re], axis=1),
        ]
    )
    return inner, outer.reshape(2, 4, 16, 2 * DIRS)


def first_tables():
    source = np.arange(4)[:, None, None]
    group = np.arange(8)[None, :, None]
    low = np.arange(8)[None, None, :]
    places = 32 * group + 8 * source + low
    cosine, sine = numpy_turns(np.arange(SIDE), places.reshape(-1), SIDE)
    shape = (SIDE, 4, 8, 8)
    cosine = cosine.reshape(shape) / 16.0
    sine = sine.reshape(shape) / 16.0
    upper = np.stack([cosine, sine], axis=3)
    lower = np.stack([-sine, cosine], axis=3)
    table = np.concatenate([upper, lower], axis=0).reshape(2 * SIDE, 4, 128)
    return jnp.asarray(table.transpose(1, 0, 2), dtype=jnp.bfloat16)


def second_table():
    cosine, sine = numpy_turns(np.arange(SIDE), np.arange(SIDE), SIDE)
    table = np.block([[cosine, sine], [-sine, cosine]]) / 16.0
    return jnp.asarray(table.reshape(2, SIDE, 2 * SIDE), dtype=jnp.bfloat16)


def twist_tables():
    cosine, sine = numpy_turns(np.arange(SIDE), np.arange(SIDE), SIDE * SIDE)
    return jnp.asarray(cosine, dtype=jnp.float32), jnp.asarray(-sine, dtype=jnp.float32)


def to_rows(flat):
    rows = flat.shape[0] // (16 * SIDE) * 8
    tiles = flat.reshape(rows // 8, SIDE, 2, 8, 128)
    return tiles.transpose(0, 3, 1, 2, 4).reshape(rows, SIDE * SIDE)


def hogel_groups():
    return [[4 * row + at for row in HOGEL_ORDER] for at in range(4)]


def per_device(views, phases, kernel_phase):
    sent = regroup(views)
    rays = lax.all_to_all(
        sent, VIEW + COL, 0, 0, axis_index_groups=hogel_groups(), tiled=True
    )
    angles = phases.astype(jnp.float32) * (2.0 * math.pi / PHASES)
    phase_cos = jnp.tile(jnp.cos(angles), (1, 2))
    phase_sin = jnp.tile(jnp.sin(angles), (1, 2))
    inner, outer = inner_outer_tables()
    me = lax.axis_index("zl") * 2 + lax.axis_index("xl")
    partners = [me ^ d for d in range(4)]
    pick = lambda table, at, axis: lax.dynamic_index_in_dim(table, at, axis, False)
    outer = jnp.stack([pick(outer, at, 1) for at in partners], axis=1)
    source_tables = first_tables()
    first = jnp.concatenate([pick(source_tables, at, 0) for at in partners], axis=1)
    twist_re, twist_im = twist_tables()
    turn = kernel_phase.reshape(SIDE, SIDE)
    tables = (first, twist_re, twist_im, second_table(), jnp.cos(turn), jnp.sin(turn))
    parts = []
    for rows, starts in (((0, 8), (0, 4, 8)), ((8, 12), (0, 8)), ((12, 16), (0, 8))):
        outer_part = outer[:, :, rows[0] : rows[1]].reshape(-1, 2 * DIRS)
        pieces = [[] for _ in range(4)]
        for start, end in zip(starts[:-1], starts[1:]):
            sending = fields(
                rays, phase_cos, phase_sin, inner, outer_part, start, end - start
            )
            pieces[0].append(sending[0])
            for d in (3, 1, 2):
                swaps = [(i, i ^ d) for i in range(4)]
                pieces[d].append(lax.ppermute(sending[d], SQUARE, swaps))
        parts.append([p for partner in pieces for p in partner])
    filled = spectra(parts[0], tables, 0)
    early = spectra(parts[1], tables, None)
    flat_re, flat_im = spectra(parts[2], tables, 1, early, filled)
    return to_rows(flat_re), to_rows(flat_im)


def solution(mesh):
    fine = Mesh(mesh.devices.reshape(2, 2, 4, 2, 2, 2), VIEW + COL)
    in_specs = (P(VIEW, COL, None), P(), P())
    out_specs = (P(VIEW + COL, None), P(VIEW + COL, None))
    return jax.shard_map(
        per_device, mesh=fine, in_specs=in_specs, out_specs=out_specs, check_vma=False
    )
```

```python
import functools
import math

import jax
import jax.numpy as jnp
import numpy as np
from jax import lax
from jax.experimental import pallas as pl
from jax.experimental.pallas import tpu as pltpu
from jax.sharding import Mesh
from jax.sharding import PartitionSpec as P

PHASES = 256
DIRS = 64
SIDE = 256
VIEW = ("xh", "co")
COL = ("y", "zh", "zl", "xl")
HOGEL_ORDER = (
    29, 20, 7, 6, 26, 28, 24, 11, 19, 14, 3, 9, 21, 30, 12, 27,
    0, 31, 23, 13, 5, 1, 8, 2, 10, 22, 15, 18, 16, 17, 4, 25,
)
RANK_OF = tuple(HOGEL_ORDER.index(row) for row in range(len(HOGEL_ORDER)))
SQUARE = ("zl", "xl")
VMEM_BYTES = 40 * 1024 * 1024


def direction_table(length):
    positions = jnp.arange(length, dtype=jnp.int32)
    angles = (positions[:, None] * positions[None, :] % length).astype(jnp.float32) * (
        2.0 * math.pi / length
    )
    factor = 1.0 / math.sqrt(length)
    return (
        (jnp.cos(angles) * factor).astype(jnp.bfloat16),
        (jnp.sin(angles) * factor).astype(jnp.bfloat16),
    )


def numpy_turns(first, second, modulus):
    angles = (np.outer(first, second) % modulus) * (2.0 * np.pi / modulus)
    return np.cos(angles), np.sin(angles)


def params(limit=VMEM_BYTES):
    return pltpu.CompilerParams(
        dimension_semantics=("arbitrary",), vmem_limit_bytes=limit
    )


def regroup_kernel(views_ref, out_ref):
    dirs, cols, lanes = views_ref.shape
    for pair in range(lanes // 128):
        block = jnp.swapaxes(views_ref[:, :, 128 * pair : 128 * (pair + 1)], 0, 1)
        for col in range(0, cols, 2):
            even, odd = block[col], block[col + 1]
            place = slice(64 * col, 64 * col + 128)
            for side in range(2):
                own = slice(64 * side, 64 * (side + 1))
                joined = jnp.concatenate([even[:, own], odd[:, own]], axis=1)
                out_ref[RANK_OF[2 * pair + side], :, place] = joined


def regroup(views, steps=2):
    dirs, cols, merged = views.shape
    each = cols // steps
    return pl.pallas_call(
        regroup_kernel,
        grid=(steps,),
        in_specs=[pl.BlockSpec((dirs, each, merged), lambda i: (0, i, 0))],
        out_specs=pl.BlockSpec((merged // 64, dirs, each * 64), lambda i: (0, 0, i)),
        out_shape=jax.ShapeDtypeStruct((merged // 64, dirs, cols * 64), jnp.bfloat16),
        compiler_params=params(60 * 1024 * 1024),
        name="regroup",
    )(views)


def field_kernel(
    start, groups, step, rays_ref, cos_ref, sin_ref, inner_ref, outer_ref, *out_refs
):
    phase_cos = cos_ref[...]
    phase_sin = sin_ref[...]
    inner = inner_ref[...]
    outer = outer_ref[...]
    count = outer.shape[0] // 2
    each = count // 4

    def partials(group):
        own = [rays_ref[RANK_OF[8 * view + start + group]] for view in range(4)]
        rays = jnp.concatenate(own, axis=0)

        def wave(tile):
            amplitude = rays[:, 128 * tile : 128 * (tile + 1)].astype(jnp.float32)
            wave_re = (amplitude * phase_cos).astype(jnp.bfloat16)
            wave_im = (amplitude * phase_sin).astype(jnp.bfloat16)
            return jnp.concatenate([wave_re, wave_im], axis=1)

        parts = []
        for low in range(8):
            waves = jnp.concatenate([wave(2 * low), wave(2 * low + 1)], axis=0)
            part = jnp.dot(waves, inner, preferred_element_type=jnp.float32)
            parts.append(part.astype(jnp.bfloat16))
        return parts

    for begin in range(0, groups, step):
        stacked = []
        for group in range(begin, begin + step):
            for part in partials(group):
                left = jnp.concatenate([part[:DIRS, :128], part[:DIRS, 128:]], axis=0)
                right = jnp.concatenate([part[DIRS:, :128], part[DIRS:, 128:]], axis=0)
                stacked.append(jnp.concatenate([left, right], axis=1))
        field = [jnp.dot(outer, s, preferred_element_type=jnp.float32) for s in stacked]
        for at in range(step):
            own = field[8 * at : 8 * (at + 1)]
            sides = []
            for rows in (slice(0, count), slice(count, 2 * count)):
                sides.append(jnp.swapaxes(jnp.stack([f[rows] for f in own]), 0, 1))
            block = jnp.concatenate(sides, axis=1).astype(jnp.bfloat16)
            for partner in range(4):
                out_refs[partner][begin + at] = block[each * partner : each * (partner + 1)]


def fields(rays, phase_cos, phase_sin, inner, outer, start, groups, step=4):
    each = outer.shape[0] // 8
    in_vmem = pl.BlockSpec(memory_space=pltpu.VMEM)
    out_shape = jax.ShapeDtypeStruct((groups, each, 16, 256), jnp.bfloat16)
    return pl.pallas_call(
        functools.partial(field_kernel, start, groups, step),
        in_specs=[in_vmem] * 5,
        out_specs=[in_vmem] * 4,
        out_shape=[out_shape] * 4,
        compiler_params=pltpu.CompilerParams(vmem_limit_bytes=VMEM_BYTES),
        cost_estimate=pl.CostEstimate(
            flops=2 * 10**9, bytes_accessed=4 * 2**20, transcendentals=0
        ),
        name="fields",
    )(rays, phase_cos, phase_sin, inner, outer)


def spectrum_kernel(count, early, filled, keep, *refs):
    pieces, tables = refs[:count], refs[count : count + 6]
    first_ref, twist_re_ref, twist_im_ref, second_ref, turn_re_ref, turn_im_ref = tables
    early_refs = refs[count + 6 : count + 6 + early]
    re_ref, im_ref, turned_ref = refs[count + 6 + early + filled :]
    rows = turned_ref.shape[0]
    half = SIDE // 2

    @pl.when(pl.program_id(0) == 0)
    def _():
        for row in range(rows):
            signal = [p[:, row].reshape(-1, SIDE) for p in pieces]
            signal = jnp.concatenate(signal, axis=0)
            section = jnp.dot(first_ref[...], signal, preferred_element_type=jnp.float32)
            section_re, section_im = section[:SIDE], section[SIDE:]
            twist_re, twist_im = twist_re_ref[...], twist_im_ref[...]
            turned_re = section_re * twist_re - section_im * twist_im
            turned_im = section_re * twist_im + section_im * twist_re
            turned_ref[row, :, :SIDE] = turned_re.astype(jnp.bfloat16)
            turned_ref[row, :, SIDE:] = turned_im.astype(jnp.bfloat16)

    def place_row(row, out_re, out_im):
        for side in range(2):
            lanes = slice(128 * side, 128 * (side + 1))
            place = pl.ds(8 * side + row, half, stride=16)
            re_ref[place, :] = out_re[:, lanes]
            im_ref[place, :] = out_im[:, lanes]

    second = second_ref[...].reshape(2 * half, 2 * SIDE)
    for row in range(rows):
        final = lax.dot_general(
            second,
            turned_ref[row],
            (((1,), (1,)), ((), ())),
            preferred_element_type=jnp.float32,
        )
        final_re, final_im = final[:half], final[half:]
        turn_re, turn_im = turn_re_ref[...], turn_im_ref[...]
        out_re = final_re * turn_re - final_im * turn_im
        out_im = final_re * turn_im + final_im * turn_re
        if keep:
            re_ref[row] = out_re
            im_ref[row] = out_im
        else:
            place_row(8 - rows + row, out_re, out_im)
    if early:
        for row in range(8 - rows):
            place_row(row, early_refs[0][row], early_refs[1][row])


def spectra(pieces, tables, half, early=(), filled=()):
    count, rows = len(pieces), pieces[0].shape[1]
    keep = half is None
    whole = lambda i: (0, 0)
    piece_specs = [pl.BlockSpec(p.shape, lambda i: (0, 0, 0, 0)) for p in pieces]
    square = pl.BlockSpec((SIDE, SIDE), whole)
    first = pl.BlockSpec((2 * SIDE, 2 * SIDE), whole)
    second = pl.BlockSpec((2, SIDE // 2, 2 * SIDE), lambda i: (0, i, 0))
    turn = pl.BlockSpec((SIDE // 2, SIDE), lambda i: (i, 0))
    kept_spec = lambda n: pl.BlockSpec((n, SIDE // 2, SIDE), lambda i: (0, i, 0))
    if keep:
        out_block = kept_spec(rows)
        out_shape = jax.ShapeDtypeStruct((rows, SIDE, SIDE), jnp.float32)
    else:
        out_block = pl.BlockSpec((8 * SIDE, 128), lambda i: (2 * half + i, 0))
        out_shape = jax.ShapeDtypeStruct((2 * 16 * SIDE, 128), jnp.float32)
    aliases = {count + 6 + len(early) + i: i for i in range(len(filled))}
    return pl.pallas_call(
        functools.partial(spectrum_kernel, count, len(early), len(filled), keep),
        grid=(2,),
        in_specs=piece_specs
        + [first, square, square, second, turn, turn]
        + [kept_spec(8 - rows)] * len(early)
        + [pl.BlockSpec(memory_space=pl.ANY)] * len(filled),
        out_specs=[out_block, out_block],
        out_shape=[out_shape, out_shape],
        scratch_shapes=[pltpu.VMEM((rows, SIDE, 2 * SIDE), jnp.bfloat16)],
        input_output_aliases=aliases,
        compiler_params=params(),
        cost_estimate=pl.CostEstimate(
            flops=10**9 * rows, bytes_accessed=2**20 * rows, transcendentals=0
        ),
        name="spectra",
    )(*pieces, *tables, *early, *filled)


def inner_outer_tables():
    table_re, table_im = direction_table(DIRS)
    zero = jnp.zeros_like(table_re)
    twice = lambda t: jnp.block([[t, zero], [zero, t]])
    inner = jnp.block(
        [[twice(table_re), twice(table_im)], [twice(-table_im), twice(table_re)]]
    )
    outer = jnp.stack(
        [
            jnp.concatenate([table_re, -table_im], axis=1),
            jnp.concatenate([table_im, table_re], axis=1),
        ]
    )
    return inner, outer.reshape(2, 4, 16, 2 * DIRS)


def first_tables():
    source = np.arange(4)[:, None, None]
    group = np.arange(8)[None, :, None]
    low = np.arange(8)[None, None, :]
    places = 32 * group + 8 * source + low
    cosine, sine = numpy_turns(np.arange(SIDE), places.reshape(-1), SIDE)
    shape = (SIDE, 4, 8, 8)
    cosine = cosine.reshape(shape) / 16.0
    sine = sine.reshape(shape) / 16.0
    upper = np.stack([cosine, sine], axis=3)
    lower = np.stack([-sine, cosine], axis=3)
    table = np.concatenate([upper, lower], axis=0).reshape(2 * SIDE, 4, 128)
    return jnp.asarray(table.transpose(1, 0, 2), dtype=jnp.bfloat16)


def second_table():
    cosine, sine = numpy_turns(np.arange(SIDE), np.arange(SIDE), SIDE)
    table = np.block([[cosine, sine], [-sine, cosine]]) / 16.0
    return jnp.asarray(table.reshape(2, SIDE, 2 * SIDE), dtype=jnp.bfloat16)


def twist_tables():
    cosine, sine = numpy_turns(np.arange(SIDE), np.arange(SIDE), SIDE * SIDE)
    return jnp.asarray(cosine, dtype=jnp.float32), jnp.asarray(-sine, dtype=jnp.float32)


def to_rows(flat):
    rows = flat.shape[0] // (16 * SIDE) * 8
    tiles = flat.reshape(rows // 8, SIDE, 2, 8, 128)
    return tiles.transpose(0, 3, 1, 2, 4).reshape(rows, SIDE * SIDE)


def hogel_groups():
    return [[4 * row + at for row in HOGEL_ORDER] for at in range(4)]


def per_device(views, phases, kernel_phase):
    sent = regroup(views)
    rays = lax.all_to_all(
        sent, VIEW + COL, 0, 0, axis_index_groups=hogel_groups(), tiled=True
    )
    angles = phases.astype(jnp.float32) * (2.0 * math.pi / PHASES)
    phase_cos = jnp.tile(jnp.cos(angles), (1, 2))
    phase_sin = jnp.tile(jnp.sin(angles), (1, 2))
    inner, outer = inner_outer_tables()
    me = lax.axis_index("zl") * 2 + lax.axis_index("xl")
    partners = [me ^ d for d in range(4)]
    pick = lambda table, at, axis: lax.dynamic_index_in_dim(table, at, axis, False)
    outer = jnp.stack([pick(outer, at, 1) for at in partners], axis=1)
    source_tables = first_tables()
    first = jnp.concatenate([pick(source_tables, at, 0) for at in partners], axis=1)
    twist_re, twist_im = twist_tables()
    turn = kernel_phase.reshape(SIDE, SIDE)
    tables = (first, twist_re, twist_im, second_table(), jnp.cos(turn), jnp.sin(turn))
    parts = []
    for rows, starts in (((0, 8), (0, 4, 8)), ((8, 12), (0, 8)), ((12, 16), (0, 8))):
        outer_part = outer[:, :, rows[0] : rows[1]].reshape(-1, 2 * DIRS)
        pieces = [[] for _ in range(4)]
        for start, end in zip(starts[:-1], starts[1:]):
            sending = fields(
                rays, phase_cos, phase_sin, inner, outer_part, start, end - start
            )
            pieces[0].append(sending[0])
            for d in (3, 1, 2):
                swaps = [(i, i ^ d) for i in range(4)]
                pieces[d].append(lax.ppermute(sending[d], SQUARE, swaps))
        parts.append([p for partner in pieces for p in partner])
    filled = spectra(parts[0], tables, 0)
    early = spectra(parts[1], tables, None)
    flat_re, flat_im = spectra(parts[2], tables, 1, early, filled)
    return to_rows(flat_re), to_rows(flat_im)


def solution(mesh):
    fine = Mesh(mesh.devices.reshape(2, 2, 4, 2, 2, 2), VIEW + COL)
    in_specs = (P(VIEW, COL, None), P(), P())
    out_specs = (P(VIEW + COL, None), P(VIEW + COL, None))
    return jax.shard_map(
        per_device, mesh=fine, in_specs=in_specs, out_specs=out_specs, check_vma=False
    )
```
